512 devices in a mesh: fsdp: 32 (over y, x), blk: 16 (over z, core).
Axes of the slice: x: 4, y: 8, z: 8, core: 2. Of those that a mesh axis runs over, the one named last changes fastest.
Arguments:
- out_grad: bfloat16 [6144, 8192], P('fsdp'), may hold values from -6 to 6
- layer_input: bfloat16 [6144, 8192], P('fsdp', 'blk'), may hold values from -6 to 6
- gate_pre: bfloat16 [6144, 14336], P('fsdp', 'blk'), may hold values from -8 to 8
- up_pre: bfloat16 [6144, 14336], P('fsdp', 'blk'), may hold values from -6 to 6
- down_weight: bfloat16 [14336, 8192], P('blk', 'fsdp'), may hold values from -0.0625 to 0.0625
- proj_hidden: bfloat16 [14336, 64], P('blk'), may hold values from -0.046875 to 0.046875
- proj_model: bfloat16 [8192, 128], P('blk'), may hold values from -0.0625 to 0.0625
- example_ids: int32 [32, 192], P('fsdp'), may hold values from 0 to 1, as said below
Outputs:
- down_scores: float32 [64, 8192], P('fsdp', 'blk')
- up_scores: float32 [64, 8192], P('fsdp', 'blk')
The draws below stay inside these ranges and needn't reach their ends.
Inputs may be any that keep to these rules, and one draw needn't show every extreme that they name: `example_ids`: within each row the example number never falls, and each of the 2 examples holds 48 to 144 neighbouring tokens; in some row one example holds exactly 144.
All inputs are finite; a program needn't handle non-finite values.
Results may differ from the reference program's by a relative error of at most 0.0029.
Values may be sent and summed in bfloat16 or wider, within the bound.
No kernel may reach another device: no remote copies, remote signals or barrier semaphores. Data moves between devices by JAX's collectives and lax.ppermute only.
A program may use at most 64 MiB of HBM per device.

```python
import jax
import jax.numpy as jnp
from jax import lax

D = 8192
HID = 14336
KH = 64
KM = 128
TOK_DEV = 192
EX_DEV = 2
TOKENS = 6144
N_FSDP = 32


def draw_example_ids(key, part):
    key = jax.random.fold_in(key, 7)
    key_first, key_row, key_side = jax.random.split(key, 3)
    longest = TOK_DEV * 3 // 4
    shortest = TOK_DEV - longest
    boundary = jax.random.randint(key_first, (N_FSDP,), shortest, longest + 1, dtype=jnp.int32)
    chosen_row = jax.random.randint(key_row, (), 0, N_FSDP, dtype=jnp.int32)
    chosen_side = jax.random.randint(key_side, (), 0, 2, dtype=jnp.int32)
    forced = jnp.where(chosen_side == 0, longest, shortest).astype(jnp.int32)
    rows = jnp.arange(N_FSDP, dtype=jnp.int32)
    boundary = jnp.where(rows == chosen_row, forced, boundary)
    positions = jnp.arange(TOK_DEV, dtype=jnp.int32)
    return (positions[None, :] >= boundary[:, None]).astype(jnp.int32)


def block_scale(own_key, extent, cuts, low, largest):
    gain, own = 1.0, jax.random.fold_in(own_key, 6)
    for position, shards_of in cuts:
        draws = jnp.exp(jax.random.uniform(jax.random.fold_in(own, position), (shards_of,), jnp.float32, low / len(cuts), largest / len(cuts)))
        gain = gain * jnp.repeat(draws, extent[position] // shards_of).reshape([-1 if axis == position else 1 for axis in range(len(extent))])
    return gain


def centred(own_key, dims, spread, most, pieces=(), held_as=jnp.bfloat16):
    drawn = spread * jax.random.normal(own_key, dims, jnp.float32)
    if pieces:
        drawn = drawn * block_scale(own_key, dims, pieces, -0.22, 0.18)
    return jnp.clip(drawn, -most, most).astype(held_as)


def setup_inputs(seed: int = 0) -> dict:
    key_of = jax.random.split(jax.random.key(seed), 9)
    return {
        "out_grad": centred(key_of[0], (TOKENS, D), 1.0, 6.0, ((0, 32),)),
        "layer_input": centred(key_of[1], (TOKENS, D), 1.0, 6.0, ((0, 32), (1, 16))),
        "gate_pre": centred(key_of[2], (TOKENS, HID), 1.5, 8.0, ((0, 32), (1, 16))),
        "up_pre": centred(key_of[3], (TOKENS, HID), 1.0, 6.0, ((0, 32), (1, 16))),
        "down_weight": centred(key_of[4], (HID, D), D ** -0.5, 0.0625, ((0, 16), (1, 32))),
        "proj_hidden": centred(key_of[5], (HID, KH), HID ** -0.5, 0.046875, ((0, 16),)),
        "proj_model": centred(key_of[6], (D, KM), D ** -0.5, 0.0625, ((0, 16),)),
        "example_ids": draw_example_ids(jax.random.fold_in(key_of[8], 71), 0),
    }


def per_example(left, right, example_ids):
    left = left.reshape(N_FSDP, TOK_DEV, left.shape[1])
    right = right.reshape(N_FSDP, TOK_DEV, right.shape[1])
    onehot = (example_ids[:, :, None] == jnp.arange(EX_DEV, dtype=jnp.int32)[None, None, :]).astype(jnp.float32)
    weighted = onehot[:, :, :, None] * left[:, :, None, :]
    scores = jnp.einsum("ntek,ntm->nekm", weighted, right, precision=lax.Precision.HIGHEST)
    return scores.reshape(N_FSDP * EX_DEV, left.shape[2] * right.shape[2])


def reference(out_grad, layer_input, gate_pre, up_pre, down_weight, proj_hidden, proj_model, example_ids):
    silu_gate = jax.nn.silu(gate_pre.astype(jnp.float32))
    hidden = (silu_gate * up_pre.astype(jnp.float32)).astype(jnp.bfloat16)
    grad_hidden = jnp.dot(out_grad, down_weight.T, preferred_element_type=jnp.float32)
    grad_up = (grad_hidden * silu_gate).astype(jnp.bfloat16)
    hid_side = jnp.dot(hidden, proj_hidden, preferred_element_type=jnp.float32)
    up_side = jnp.dot(grad_up, proj_hidden, preferred_element_type=jnp.float32)
    grad_side = jnp.dot(out_grad, proj_model, preferred_element_type=jnp.float32)
    input_side = jnp.dot(layer_input, proj_model, preferred_element_type=jnp.float32)
    down_scores = per_example(hid_side, grad_side, example_ids)
    up_scores = per_example(up_side, input_side, example_ids)
    return down_scores, up_scores
```

```python
import jax
import jax.numpy as jnp
from jax import lax
from jax.sharding import Mesh
from jax.sharding import PartitionSpec as P

NY, NX, NZ, NC = 8, 4, 8, 2
NB = NZ * NC
ZC = ("z", "core")
BF16, F32 = jnp.bfloat16, jnp.float32


def turn(n, step):
    return [(i, (i + step) % n) for i in range(n)]


def dot_nt(a, b, **kw):
    return lax.dot_general(a, b, (((1,), (1,)), ((), ())), preferred_element_type=F32, **kw)


def dot_tt(a, b, **kw):
    return lax.dot_general(a, b, (((0,), (1,)), ((), ())), preferred_element_type=F32, **kw)


def on_device(out_grad, layer_input, gate_pre, up_pre, down_weight, proj_hidden, proj_model, example_ids):
    y, x, core = lax.axis_index("y"), lax.axis_index("x"), lax.axis_index("core")
    blk = lax.axis_index(ZC)
    tok, hid = gate_pre.shape
    wide = down_weight.shape[1]
    half = hid // 2

    def cols(shift_y, at_x):
        block = lax.rem(y - shift_y + NY, NY) * NX + at_x
        return lax.dynamic_slice_in_dim(out_grad, block * wide, wide, 1)

    up1 = lax.ppermute(down_weight, "y", turn(NY, 1))
    dn1 = lax.ppermute(down_weight, "y", turn(NY, -1))
    got = []
    for s in (2, 1, 3):
        at_x = lax.rem(x + s, NX)
        piece = jnp.concatenate([gate_pre] + [cols(core * 4 + j, at_x) for j in range(4)], axis=1)
        got.append((s, lax.ppermute(piece, "x", turn(NX, s))))
    got = [g for _, g in sorted(got, key=lambda p: p[0])]
    up2 = lax.ppermute(up1, "y", turn(NY, 1))
    dn2 = lax.ppermute(dn1, "y", turn(NY, -1))
    mine = jnp.stack([g[:, hid:] for g in got])
    other = lax.ppermute(mine, "core", turn(NC, 1))
    up3 = lax.ppermute(up2, "y", turn(NY, 1))
    dn3 = lax.ppermute(dn2, "y", turn(NY, -1))
    far_a = lax.ppermute(up3[:half], "y", turn(NY, 1))
    far_b = lax.ppermute(dn3[half:], "y", turn(NY, -1))

    feat = layer_input.shape[1]
    grad_cols = lax.dynamic_slice_in_dim(out_grad, blk * feat, feat, 1)
    grad_part = dot_tt(proj_model, grad_cols)
    input_part = dot_tt(proj_model, layer_input)
    hidden = (jax.nn.silu(gate_pre.astype(F32)) * up_pre.astype(F32)).astype(BF16)
    hid_part = dot_tt(proj_hidden, hidden)
    early = jnp.concatenate(
        [jnp.concatenate([grad_part, input_part], 0).reshape(NB, -1, tok), hid_part.reshape(NB, -1, tok)], axis=1
    )
    early = jnp.sum(lax.all_to_all(early, ZC, 0, 0), axis=0)
    n_side = 2 * proj_model.shape[1] // NB
    sides = lax.all_to_all(jnp.broadcast_to(early[None, :n_side], (NB, n_side, tok)), ZC, 0, 0).reshape(2, -1, tok)
    hid_side = early[n_side:]

    gates = [gate_pre] + [g[:, :hid] for g in got]
    low = jnp.where(core == 0, mine, other)
    high = jnp.where(core == 0, other, mine)
    grads = [jnp.concatenate([jnp.concatenate([cols(j, x) for j in range(8)], 1)] , 1)]
    grads += [jnp.concatenate([low[i], high[i]], 1) for i in range(3)]
    grads = jnp.concatenate(grads, 0)
    weights = jnp.concatenate(
        [down_weight, up1, up2, up3, jnp.concatenate([far_a, far_b], 0), dn3, dn2, dn1], 1
    )
    grad_hidden = dot_nt(grads, weights)
    silu_gate = jax.nn.silu(jnp.concatenate(gates, 0).astype(F32))
    grad_up = (grad_hidden * silu_gate).astype(BF16)
    up_part = dot_nt(proj_hidden.T, grad_up)
    up_part = [up_part[:, s * tok : (s + 1) * tok] for s in range(NX)]
    back = up_part[0]
    for s in (2, 1, 3):
        back = back + lax.ppermute(up_part[s], "x", turn(NX, -s))
    up_side = jnp.sum(lax.all_to_all(back.reshape(NB, -1, tok), ZC, 0, 0), axis=0)

    picks = (example_ids == jnp.arange(2, dtype=jnp.int32)[:, None]).astype(F32)

    def scores(left, right):
        picked = (picks[:, None, :] * left[None]).reshape(-1, tok)
        return dot_nt(picked, right, precision=lax.Precision.HIGHEST).reshape(2, -1)

    return scores(hid_side, sides[0]), scores(up_side, sides[1])


def solution(mesh):
    fine = Mesh(mesh.devices.reshape(NY, NX, NZ, NC), ("y", "x", "z", "core"))
    yx = ("y", "x")
    in_specs = (P(yx, None), P(yx, ZC), P(yx, ZC), P(yx, ZC), P(ZC, yx), P(ZC, None), P(ZC, None), P(yx, None))
    out_specs = (P(yx, ZC), P(yx, ZC))
    return jax.shard_map(on_device, mesh=fine, in_specs=in_specs, out_specs=out_specs, check_vma=False)
```

```python
import functools

import jax
import jax.numpy as jnp
from jax import lax
from jax.experimental import pallas as pl
from jax.experimental.pallas import tpu as pltpu
from jax.sharding import Mesh
from jax.sharding import PartitionSpec as P

NY, NX, NZ, NC = 8, 4, 8, 2
NB = NZ * NC
ZC = ("z", "core")
BF16, F32 = jnp.bfloat16, jnp.float32
ANY = pl.BlockSpec(memory_space=pl.ANY)
SMEM = pl.BlockSpec(memory_space=pltpu.SMEM)


def turn(n, step):
    return [(i, (i + step) % n) for i in range(n)]


def dot_nt(a, b, **kw):
    return lax.dot_general(a, b, (((1,), (1,)), ((), ())), preferred_element_type=F32, **kw)


def dot_tt(a, b, **kw):
    return lax.dot_general(a, b, (((0,), (1,)), ((), ())), preferred_element_type=F32, **kw)


def pack_kernel(place, grad, gate, *rest):
    outs, sems = rest[:-1], rest[-1]
    hid = gate.shape[1]
    wide = (outs[0].shape[1] - hid) // NY
    y, x = place[0], place[1]
    copies = []
    for s, out in enumerate(outs):
        at = lax.rem(x + s + 1, NX)
        copies.append(pltpu.make_async_copy(gate, out.at[:, pl.ds(0, hid)], sems.at[s, NY]))
        for i in range(NY):
            start = pl.multiple_of((lax.rem(y - i + NY, NY) * NX + at) * wide, wide)
            copies.append(
                pltpu.make_async_copy(
                    grad.at[:, pl.ds(start, wide)], out.at[:, pl.ds(hid + i * wide, wide)], sems.at[s, i]
                )
            )
    for c in copies:
        c.start()
    for c in copies:
        c.wait()


def pack(place, grad, gate, wide):
    tok, hid = gate.shape
    out = jax.ShapeDtypeStruct((tok, hid + NY * wide), BF16)
    return pl.pallas_call(
        pack_kernel,
        out_shape=[out] * (NX - 1),
        in_specs=[SMEM, ANY, ANY],
        out_specs=[ANY] * (NX - 1),
        scratch_shapes=[pltpu.SemaphoreType.DMA((NX - 1, NY + 1))],
        cost_estimate=pl.CostEstimate(flops=0, bytes_accessed=7_000_000, transcendentals=0),
        name="pack",
    )(place, grad, gate)


def main_kernel(place, grad, gates_own, x1, x2, x3, w0, w1, w2, w3, far_a, far_b, w5, w6, w7, proj, out, g, gate, w, g_sem, w_sem):
    y, x = place[0], place[1]
    nx, tok, hid = gate.shape
    wide = w0.shape[1]
    half = hid // 2
    copies = [pltpu.make_async_copy(gates_own, gate.at[0], g_sem.at[0, NY])]
    for i in range(NY):
        start = pl.multiple_of((lax.rem(y - i + NY, NY) * NX + x) * wide, wide)
        copies.append(
            pltpu.make_async_copy(grad.at[:, pl.ds(start, wide)], g.at[0, :, pl.ds(i * wide, wide)], g_sem.at[0, i])
        )
    for s, got in enumerate((x1, x2, x3)):
        copies.append(pltpu.make_async_copy(got.at[:, pl.ds(0, hid)], gate.at[s + 1], g_sem.at[s + 1, 0]))
        copies.append(pltpu.make_async_copy(got.at[:, pl.ds(hid, NY * wide)], g.at[s + 1], g_sem.at[s + 1, 1]))
    for i, src in enumerate((w0, w1, w2, w3, None, w5, w6, w7)):
        if src is None:
            copies.append(
                pltpu.make_async_copy(far_a, w.at[pl.ds(0, half), pl.ds(i * wide, wide)], w_sem.at[i])
            )
            copies.append(
                pltpu.make_async_copy(far_b, w.at[pl.ds(half, half), pl.ds(i * wide, wide)], w_sem.at[NY])
            )
        else:
            copies.append(pltpu.make_async_copy(src, w.at[:, pl.ds(i * wide, wide)], w_sem.at[i]))
    for c in copies:
        c.start()
    for c in copies:
        c.wait()
    grads = g[...].reshape(nx * tok, NY * wide)
    gates = gate[...].reshape(nx * tok, hid)
    total = None
    start = 0
    while start < hid:
        size = min(256, hid - start)
        gh = dot_nt(grads, w[start : start + size, :])
        gp = gates[:, start : start + size].astype(F32)
        gu = gh * (gp / (1.0 + jnp.exp(-gp)))
        hi = gu.astype(BF16)
        lo = (gu - hi.astype(F32)).astype(BF16)
        p = proj[:, start : start + size]
        part = dot_nt(p, hi) + dot_nt(p, lo)
        total = part if total is None else total + part
        start += size
    per = total.shape[0] // NB
    for j in range(nx):
        to = lax.rem(x - j + nx, nx)
        for b in range(NB):
            out[to, b] = total[b * per : (b + 1) * per, j * tok : (j + 1) * tok]


def main(place, grad, gate, got, shards, proj):
    tok, hid = gate.shape
    wide = shards[0].shape[1]
    per = proj.shape[0] // NB
    macs = NX * tok * hid * (NY * wide + proj.shape[0])
    return pl.pallas_call(
        main_kernel,
        out_shape=jax.ShapeDtypeStruct((NX, NB, per, tok), F32),
        in_specs=[SMEM] + [ANY] * 14 + [pl.BlockSpec(memory_space=pltpu.VMEM)],
        out_specs=pl.BlockSpec(memory_space=pltpu.VMEM),
        scratch_shapes=[
            pltpu.VMEM((NX, tok, NY * wide), BF16),
            pltpu.VMEM((NX, tok, hid), BF16),
            pltpu.VMEM((hid, NY * wide), BF16),
            pltpu.SemaphoreType.DMA((NX, NY + 1)),
            pltpu.SemaphoreType.DMA((NY + 1,)),
        ],
        compiler_params=pltpu.CompilerParams(vmem_limit_bytes=32 << 20),
        cost_estimate=pl.CostEstimate(flops=2 * macs, bytes_accessed=10_000_000, transcendentals=NX * tok * hid),
        name="main",
    )(place, grad, gate, *got, *shards, proj)


def on_device(out_grad, layer_input, gate_pre, up_pre, down_weight, proj_hidden, proj_model, example_ids):
    y, x = lax.axis_index("y"), lax.axis_index("x")
    blk = lax.axis_index(ZC)
    place = jnp.stack([y, x]).astype(jnp.int32)
    tok, hid = gate_pre.shape
    half = hid // 2
    feat = layer_input.shape[1]
    grad_cols = lax.dynamic_slice_in_dim(out_grad, blk * feat, feat, 1)
    grad_part = dot_tt(proj_model, grad_cols)
    input_part = dot_tt(proj_model, layer_input)
    hidden = (jax.nn.silu(gate_pre.astype(F32)) * up_pre.astype(F32)).astype(BF16)
    hid_part = dot_tt(proj_hidden, hidden)
    early = jnp.concatenate(
        [jnp.concatenate([grad_part, input_part], 0).reshape(NB, -1, tok), hid_part.reshape(NB, -1, tok)], axis=1
    )

    up1 = lax.ppermute(down_weight, "y", turn(NY, 1))
    dn1 = lax.ppermute(down_weight, "y", turn(NY, -1))
    p1, p2, p3 = pack(place, out_grad, gate_pre, down_weight.shape[1])
    up1, dn1, early = lax.optimization_barrier((up1, dn1, early))
    x1, x2, x3 = [lax.ppermute(p, "x", turn(NX, s + 1)) for s, p in enumerate((p1, p2, p3))]
    up2 = lax.ppermute(up1, "y", turn(NY, 1))
    dn2 = lax.ppermute(dn1, "y", turn(NY, -1))
    early = jnp.sum(lax.all_to_all(early, ZC, 0, 0), axis=0)
    n_side = 2 * proj_model.shape[1] // NB
    up3 = lax.ppermute(up2, "y", turn(NY, 1))
    dn3 = lax.ppermute(dn2, "y", turn(NY, -1))
    sides = lax.all_to_all(jnp.broadcast_to(early[None, :n_side], (NB, n_side, tok)), ZC, 0, 0).reshape(2, -1, tok)
    hid_side = early[n_side:]
    up3, dn3, early, x1, x3 = lax.optimization_barrier((up3, dn3, early, x1, x3))
    far_a = lax.ppermute(up3[:half], "y", turn(NY, 1))
    far_b = lax.ppermute(dn3[half:], "y", turn(NY, -1))
    x2, far_a, far_b, sides = lax.optimization_barrier((x2, far_a, far_b, sides))

    up_part = main(place, out_grad, gate_pre, (x1, x2, x3), (down_weight, up1, up2, up3, far_a, far_b, dn3, dn2, dn1), proj_hidden.T)
    up_part = jnp.sum(lax.all_to_all(up_part, "x", 0, 0), axis=0)
    up_side = jnp.sum(lax.all_to_all(up_part, ZC, 0, 0), axis=0)

    picks = (example_ids == jnp.arange(2, dtype=jnp.int32)[:, None]).astype(F32)

    def scores(left, right):
        picked = (picks[:, None, :] * left[None]).reshape(-1, tok)
        return dot_nt(picked, right, precision=lax.Precision.HIGHEST).reshape(2, -1)

    return scores(hid_side, sides[0]), scores(up_side, sides[1])


def solution(mesh):
    fine = Mesh(mesh.devices.reshape(NY, NX, NZ, NC), ("y", "x", "z", "core"))
    yx = ("y", "x")
    in_specs = (P(yx, None), P(yx, ZC), P(yx, ZC), P(yx, ZC), P(ZC, yx), P(ZC, None), P(ZC, None), P(yx, None))
    out_specs = (P(yx, ZC), P(yx, ZC))
    return jax.shard_map(on_device, mesh=fine, in_specs=in_specs, out_specs=out_specs, check_vma=False)
```

```python
import jax
import jax.numpy as jnp
from jax import lax
from jax.experimental import pallas as pl
from jax.experimental.pallas import tpu as pltpu
from jax.sharding import Mesh
from jax.sharding import PartitionSpec as P

NY, NX, NZ, NC = 8, 4, 8, 2
NB = NZ * NC
FAR = NY // 2
ZC = ("z", "core")
BF16, F32 = jnp.bfloat16, jnp.float32
HBM = pl.BlockSpec(memory_space=pltpu.HBM)
VMEM = pl.BlockSpec(memory_space=pltpu.VMEM)
SMEM = pl.BlockSpec(memory_space=pltpu.SMEM)
PARAMS = pltpu.CompilerParams(vmem_limit_bytes=40 << 20)


def turn(n, step):
    return [(i, (i + step) % n) for i in range(n)]


def dot_nt(a, b, **kw):
    return lax.dot_general(a, b, (((1,), (1,)), ((), ())), preferred_element_type=F32, **kw)


def silu(v):
    return v / (1.0 + jnp.exp(-v))


def columns(y, back, x, wide):
    return pl.multiple_of((lax.rem(y - back + NY, NY) * NX + x) * wide, wide)


def prepare_kernel(place, grad, gate, up, inp, model, hproj, p1, p2, p3, early, buf, gate_v, up_v, inp_v, gcols, model_v, hproj_v, in_sem, out_sem, side_sem):
    outs = (p1, p2, p3)
    tok, hid = gate.shape
    wide = (p1.shape[1] - hid) // NY
    feat = inp.shape[1]
    y, x, blk = place[0], place[1], place[2]
    fills, sends = [], []
    for s, out in enumerate(outs):
        at = lax.rem(x + s + 1, NX)
        fill = [pltpu.make_async_copy(gate, buf.at[s, :, pl.ds(0, hid)], in_sem.at[s, NY])]
        for i in range(NY):
            fill.append(
                pltpu.make_async_copy(
                    grad.at[:, pl.ds(columns(y, i, at, wide), wide)],
                    buf.at[s, :, pl.ds(hid + i * wide, wide)],
                    in_sem.at[s, i],
                )
            )
        fills.append(fill)
        sends.append(pltpu.make_async_copy(buf.at[s], out, out_sem.at[s]))
        for c in fill:
            c.start()
    loads = [
        pltpu.make_async_copy(gate, gate_v, side_sem.at[0]),
        pltpu.make_async_copy(up, up_v, side_sem.at[1]),
        pltpu.make_async_copy(inp, inp_v, side_sem.at[2]),
        pltpu.make_async_copy(grad.at[:, pl.ds(pl.multiple_of(blk * feat, feat), feat)], gcols, side_sem.at[3]),
        pltpu.make_async_copy(model, model_v, side_sem.at[4]),
        pltpu.make_async_copy(hproj, hproj_v, side_sem.at[5]),
    ]
    for c in loads:
        c.start()
    for fill, send in zip(fills, sends):
        for c in fill:
            c.wait()
        send.start()
    for c in loads:
        c.wait()
    hidden = (silu(gate_v[...].astype(F32)) * up_v[...].astype(F32)).astype(BF16)
    hid_side = dot_nt(hproj_v[...], hidden)
    m = model_v[...]
    parts = [jnp.dot(v[...], m, preferred_element_type=F32).T for v in (gcols, inp_v)]
    side = 2 * model.shape[1] // NB
    per = hproj.shape[0] // NB
    for b in range(NB):
        part = parts[b // (NB // 2)]
        r = (b % (NB // 2)) * side
        early[b, 0:side, :] = part[r : r + side, :]
        early[b, side : side + per, :] = hid_side[b * per : (b + 1) * per, :]
    for c in sends:
        c.wait()


def prepare(place, grad, gate, up, inp, model, hproj, wide):
    tok, hid = gate.shape
    feat = inp.shape[1]
    out = jax.ShapeDtypeStruct((tok, hid + NY * wide), BF16)
    rows = 2 * model.shape[1] // NB + hproj.shape[0] // NB
    return pl.pallas_call(
        prepare_kernel,
        out_shape=[out] * 3 + [jax.ShapeDtypeStruct((NB, rows, tok), F32)],
        in_specs=[SMEM] + [HBM] * 6,
        out_specs=[HBM] * 3 + [VMEM],
        scratch_shapes=[
            pltpu.VMEM((NX - 1, tok, hid + NY * wide), BF16),
            pltpu.VMEM((tok, hid), BF16),
            pltpu.VMEM((tok, hid), BF16),
            pltpu.VMEM((tok, feat), BF16),
            pltpu.VMEM((tok, feat), BF16),
            pltpu.VMEM(model.shape, BF16),
            pltpu.VMEM(hproj.shape, BF16),
            pltpu.SemaphoreType.DMA((NX - 1, NY + 1)),
            pltpu.SemaphoreType.DMA((NX - 1,)),
            pltpu.SemaphoreType.DMA((6,)),
        ],
        compiler_params=pltpu.CompilerParams(vmem_limit_bytes=60 << 20),
        cost_estimate=pl.CostEstimate(flops=80_000_000, bytes_accessed=8_000_000, transcendentals=tok * hid),
        name="prepare",
    )(place, grad, gate, up, inp, model, hproj)


def share_kernel(got, out, hid_side):
    total = got[0]
    for b in range(1, NB):
        total = total + got[b]
    side = out.shape[1]
    for b in range(NB):
        out[b] = total[:side]
    hid_side[...] = total[side:]


def share(got):
    _, rows, tok = got.shape
    per = rows - NB
    return pl.pallas_call(
        share_kernel,
        out_shape=[jax.ShapeDtypeStruct((NB, rows - per, tok), F32), jax.ShapeDtypeStruct((per, tok), F32)],
        in_specs=[VMEM],
        out_specs=[VMEM, VMEM],
        name="share",
    )(got)


def near_kernel(place, grad, x1, x2, x3, w0, w1, w2, w3, w5, w6, w7, acc, g, w, g_sem, w_sem):
    y, x = place[0], place[1]
    nx, tok, hid = acc.shape
    wide = w0.shape[1]
    shards = (w0, w1, w2, w3, None, w5, w6, w7)
    live = [i for i in range(NY) if i != FAR]
    copies = []
    for k, i in enumerate(live):
        copies.append(pltpu.make_async_copy(shards[i], w.at[:, pl.ds(k * wide, wide)], w_sem.at[k]))
        copies.append(
            pltpu.make_async_copy(
                grad.at[:, pl.ds(columns(y, i, x, wide), wide)], g.at[0, :, pl.ds(k * wide, wide)], g_sem.at[0, k]
            )
        )
    low = FAR * wide
    high = (NY - 1 - FAR) * wide
    for s, got in enumerate((x1, x2, x3)):
        copies.append(pltpu.make_async_copy(got.at[:, pl.ds(hid, low)], g.at[s + 1, :, pl.ds(0, low)], g_sem.at[s + 1, 0]))
        copies.append(
            pltpu.make_async_copy(
                got.at[:, pl.ds(hid + low + wide, high)], g.at[s + 1, :, pl.ds(low, high)], g_sem.at[s + 1, 1]
            )
        )
    for c in copies:
        c.start()
    for c in copies:
        c.wait()
    grads = g[...].reshape(nx * tok, len(live) * wide)
    start = 0
    while start < hid:
        size = min(256, hid - start)
        acc[:, :, start : start + size] = dot_nt(grads, w[start : start + size, :]).reshape(nx, tok, size)
        start += size


def near(place, grad, got, shards):
    tok = grad.shape[0]
    hid, wide = shards[0].shape
    k = (NY - 1) * wide
    return pl.pallas_call(
        near_kernel,
        out_shape=jax.ShapeDtypeStruct((NX, tok, hid), F32),
        in_specs=[SMEM] + [HBM] * 11,
        out_specs=VMEM,
        scratch_shapes=[
            pltpu.VMEM((NX, tok, k), BF16),
            pltpu.VMEM((hid, k), BF16),
            pltpu.SemaphoreType.DMA((NX, NY - 1)),
            pltpu.SemaphoreType.DMA((NY - 1,)),
        ],
        compiler_params=PARAMS,
        cost_estimate=pl.CostEstimate(flops=2 * NX * tok * hid * k, bytes_accessed=9_000_000, transcendentals=0),
        name="near",
    )(place, grad, *got, *shards)


def far_kernel(place, acc, grad, gate_own, x1, x2, x3, w4, proj, out, a_v, g, gate, w, p, sems):
    y, x = place[0], place[1]
    nx, tok, hid = acc.shape
    wide = w4.shape[1]
    per = proj.shape[0] // NB
    heads = [pltpu.make_async_copy(w4, w, sems.at[nx, 0]), pltpu.make_async_copy(proj, p, sems.at[nx, 1])]
    for c in heads:
        c.start()
    waits = []
    for s, got in enumerate((None, x1, x2, x3)):
        if got is None:
            mine = [
                pltpu.make_async_copy(grad.at[:, pl.ds(columns(y, FAR, x, wide), wide)], g.at[s], sems.at[s, 0]),
                pltpu.make_async_copy(gate_own, gate.at[s], sems.at[s, 1]),
            ]
        else:
            mine = [
                pltpu.make_async_copy(got.at[:, pl.ds(hid + FAR * wide, wide)], g.at[s], sems.at[s, 0]),
                pltpu.make_async_copy(got.at[:, pl.ds(0, hid)], gate.at[s], sems.at[s, 1]),
            ]
        mine.append(pltpu.make_async_copy(acc.at[s], a_v.at[s], sems.at[s, 2]))
        for c in mine:
            c.start()
        waits.append(mine)
    for c in heads:
        c.wait()
    for s in range(nx):
        for c in waits[s]:
            c.wait()
        gh = a_v[s] + dot_nt(g[s], w[...])
        gu = gh * silu(gate[s].astype(F32))
        hi = gu.astype(BF16)
        lo = (gu - hi.astype(F32)).astype(BF16)
        part = dot_nt(p[...], hi) + dot_nt(p[...], lo)
        to = lax.rem(x - s + nx, nx)
        for b in range(NB):
            out[to, b] = part[b * per : (b + 1) * per, :]


def far(place, acc, grad, gate, got, w4, proj):
    nx, tok, hid = acc.shape
    wide = w4.shape[1]
    per = proj.shape[0] // NB
    return pl.pallas_call(
        far_kernel,
        out_shape=jax.ShapeDtypeStruct((nx, NB, per, tok), F32),
        in_specs=[SMEM] + [HBM] * 8,
        out_specs=VMEM,
        scratch_shapes=[
            pltpu.VMEM((nx, tok, hid), F32),
            pltpu.VMEM((nx, tok, wide), BF16),
            pltpu.VMEM((nx, tok, hid), BF16),
            pltpu.VMEM((hid, wide), BF16),
            pltpu.VMEM(proj.shape, BF16),
            pltpu.SemaphoreType.DMA((nx + 1, 3)),
        ],
        compiler_params=PARAMS,
        cost_estimate=pl.CostEstimate(
            flops=2 * nx * tok * hid * (wide + 128), bytes_accessed=6_000_000, transcendentals=nx * tok * hid
        ),
        name="far",
    )(place, acc, grad, gate, *got, w4, proj)


def finish_kernel(got, hid_side, sides, ids, down, up):
    up_side = got[0]
    for b in range(1, got.shape[0]):
        up_side = up_side + got[b]
    half = NB // 2
    tok = ids.shape[1]
    which = ids[...]
    for left, first, out in ((hid_side[...], 0, down), (up_side, half, up)):
        right = sides[first : first + half].reshape(-1, tok)
        picked = jnp.concatenate([jnp.where(which == e, left, 0.0) for e in range(2)], axis=0)
        res = dot_nt(picked, right, precision=lax.Precision.HIGHEST)
        per, width = left.shape[0], right.shape[0]
        for e in range(2):
            for k in range(per):
                r = e * per + k
                out[e : e + 1, k * width : (k + 1) * width] = res[r : r + 1, :]


def finish(got, hid_side, sides, ids):
    per = hid_side.shape[0]
    width = sides.shape[1] * NB // 2
    out = jax.ShapeDtypeStruct((2, per * width), F32)
    return pl.pallas_call(
        finish_kernel, out_shape=[out, out], in_specs=[VMEM] * 4, out_specs=[VMEM, VMEM], name="finish"
    )(got, hid_side, sides, ids)


def on_device(out_grad, layer_input, gate_pre, up_pre, down_weight, proj_hidden, proj_model, example_ids):
    place = jnp.stack([lax.axis_index("y"), lax.axis_index("x"), lax.axis_index(ZC)]).astype(jnp.int32)
    hproj = proj_hidden.T
    up1 = lax.ppermute(down_weight, "y", turn(NY, 1))
    dn1 = lax.ppermute(down_weight, "y", turn(NY, -1))
    p1, p2, p3, early = prepare(
        place, out_grad, gate_pre, up_pre, layer_input, proj_model, hproj, down_weight.shape[1]
    )
    up1, dn1, early = lax.optimization_barrier((up1, dn1, early))
    x1, x2, x3 = [lax.ppermute(p, "x", turn(NX, s + 1)) for s, p in enumerate((p1, p2, p3))]
    up2 = lax.ppermute(up1, "y", turn(NY, 1))
    dn2 = lax.ppermute(dn1, "y", turn(NY, -1))
    early = lax.all_to_all(early, ZC, 0, 0)
    wide_sides, hid_side = share(early)
    up3 = lax.ppermute(up2, "y", turn(NY, 1))
    dn3 = lax.ppermute(dn2, "y", turn(NY, -1))
    sides = lax.all_to_all(wide_sides, ZC, 0, 0)
    up3, dn3, hid_side, x1, x3 = lax.optimization_barrier((up3, dn3, hid_side, x1, x3))
    w4 = lax.ppermute(up3, "y", turn(NY, 1))
    x2, sides = lax.optimization_barrier((x2, sides))
    acc = near(place, out_grad, (x1, x2, x3), (down_weight, up1, up2, up3, dn3, dn2, dn1))
    up_part = far(place, acc, out_grad, gate_pre, (x1, x2, x3), w4, hproj)
    up_side = lax.all_to_all(up_part.reshape((NX * NB,) + up_part.shape[2:]), ("x",) + ZC, 0, 0)
    return tuple(finish(up_side, hid_side, sides, example_ids))


def solution(mesh):
    fine = Mesh(mesh.devices.reshape(NY, NX, NZ, NC), ("y", "x", "z", "core"))
    yx = ("y", "x")
    in_specs = (P(yx, None), P(yx, ZC), P(yx, ZC), P(yx, ZC), P(ZC, yx), P(ZC, None), P(ZC, None), P(yx, None))
    out_specs = (P(yx, ZC), P(yx, ZC))
    return jax.shard_map(on_device, mesh=fine, in_specs=in_specs, out_specs=out_specs, check_vma=False)
```

```python
import jax
import jax.numpy as jnp
from jax import lax
from jax.experimental import pallas as pl
from jax.experimental.pallas import tpu as pltpu
from jax.sharding import Mesh
from jax.sharding import PartitionSpec as P

NY, NX, NZ, NC = 8, 4, 8, 2
NB = NZ * NC
FAR = NY // 2
EXTRA = 16
CHUNK = 256
ZC = ("z", "core")
BF16, F32 = jnp.bfloat16, jnp.float32
HBM = pl.BlockSpec(memory_space=pltpu.HBM)
VMEM = pl.BlockSpec(memory_space=pltpu.VMEM)
WIDE = pltpu.CompilerParams(vmem_limit_bytes=60 << 20)


def turn(n, step):
    return [(i, (i + step) % n) for i in range(n)]


def dot_nt(a, b, **kw):
    return lax.dot_general(a, b, (((1,), (1,)), ((), ())), preferred_element_type=F32, **kw)


def silu(v):
    return v / (1.0 + jnp.exp(-v))


def columns(y, back, x, wide):
    return pl.multiple_of((lax.rem(y - back + NY, NY) * NX + x) * wide, wide)


def here():
    return lax.axis_index("y"), lax.axis_index("x"), lax.axis_index("z") * NC + lax.axis_index("core")


def prepare_kernel(grad, gate, up, inp, model, hproj, p1, p2, p3, early, buf, gate_v, up_v, inp_v, gcols, model_v, hproj_v, in_sem, out_sem, side_sem):
    outs = (p1, p2, p3)
    tok, hid = gate.shape
    wide = (p1.shape[1] - hid) // NY
    feat = inp.shape[1]
    y, x, blk = here()
    fills, sends = [], []
    for s, out in enumerate(outs):
        at = lax.rem(x + s + 1, NX)
        fill = [pltpu.make_async_copy(gate, buf.at[s, :, pl.ds(0, hid)], in_sem.at[s, NY])]
        for i in range(NY):
            fill.append(
                pltpu.make_async_copy(
                    grad.at[:, pl.ds(columns(y, i, at, wide), wide)],
                    buf.at[s, :, pl.ds(hid + i * wide, wide)],
                    in_sem.at[s, i],
                )
            )
        fills.append(fill)
        sends.append(pltpu.make_async_copy(buf.at[s], out, out_sem.at[s]))
        for c in fill:
            c.start()
    loads = [
        pltpu.make_async_copy(gate, gate_v, side_sem.at[0]),
        pltpu.make_async_copy(up, up_v, side_sem.at[1]),
        pltpu.make_async_copy(inp, inp_v, side_sem.at[2]),
        pltpu.make_async_copy(grad.at[:, pl.ds(pl.multiple_of(blk * feat, feat), feat)], gcols, side_sem.at[3]),
        pltpu.make_async_copy(model, model_v, side_sem.at[4]),
        pltpu.make_async_copy(hproj, hproj_v, side_sem.at[5]),
    ]
    for c in loads:
        c.start()
    for fill, send in zip(fills, sends):
        for c in fill:
            c.wait()
        send.start()
    for c in loads:
        c.wait()
    hidden = (silu(gate_v[...].astype(F32)) * up_v[...].astype(F32)).astype(BF16)
    hid_side = dot_nt(hproj_v[...], hidden)
    high = hid_side.astype(BF16).astype(F32)
    low = hid_side - high
    m = model_v[...]
    side = jnp.concatenate(
        [jnp.dot(v[...], m, preferred_element_type=F32) for v in (gcols, inp_v)], axis=1
    ).astype(BF16)
    width = side.shape[1]
    per = hproj.shape[0] // NB
    for b in range(NB):
        early[b, 0:tok, :] = side
        rows = jnp.concatenate(
            [high[b * per : (b + 1) * per], low[b * per : (b + 1) * per], jnp.zeros((EXTRA - 2 * per, tok), F32)], axis=0
        )
        early[b, tok : tok + EXTRA, :] = jnp.concatenate(
            [rows, jnp.zeros((EXTRA, width - tok), F32)], axis=1
        ).astype(BF16)
    for c in sends:
        c.wait()


def prepare(grad, gate, up, inp, model, hproj, wide):
    tok, hid = gate.shape
    feat = inp.shape[1]
    out = jax.ShapeDtypeStruct((tok, hid + NY * wide), BF16)
    return pl.pallas_call(
        prepare_kernel,
        out_shape=[out] * 3 + [jax.ShapeDtypeStruct((NB, tok + EXTRA, 2 * model.shape[1]), BF16)],
        in_specs=[HBM] * 6,
        out_specs=[HBM] * 3 + [VMEM],
        scratch_shapes=[
            pltpu.VMEM((NX - 1, tok, hid + NY * wide), BF16),
            pltpu.VMEM((tok, hid), BF16),
            pltpu.VMEM((tok, hid), BF16),
            pltpu.VMEM((tok, feat), BF16),
            pltpu.VMEM((tok, feat), BF16),
            pltpu.VMEM(model.shape, BF16),
            pltpu.VMEM(hproj.shape, BF16),
            pltpu.SemaphoreType.DMA((NX - 1, NY + 1)),
            pltpu.SemaphoreType.DMA((NX - 1,)),
            pltpu.SemaphoreType.DMA((6,)),
        ],
        compiler_params=WIDE,
        cost_estimate=pl.CostEstimate(flops=80_000_000, bytes_accessed=8_000_000, transcendentals=tok * hid),
        name="prepare",
    )(grad, gate, up, inp, model, hproj)


def main_kernel(grad, own, x1, x2, x3, w0, w1, w2, w3, w4, w5, w6, w7, proj, out, g, gate, w, p, g_sem, w_sem):
    y, x, _ = here()
    nx, tok, hid = gate.shape
    wide = w0.shape[1]
    per = proj.shape[0] // NB
    chunks = [(c, min(CHUNK, hid - c)) for c in range(0, hid, CHUNK)]
    firsts = []
    for i in range(NY):
        firsts.append(
            pltpu.make_async_copy(
                grad.at[:, pl.ds(columns(y, i, x, wide), wide)], g.at[0, :, pl.ds(i * wide, wide)], g_sem.at[0, i]
            )
        )
    for s, got in enumerate((x1, x2, x3)):
        firsts.append(pltpu.make_async_copy(got.at[:, pl.ds(hid, NY * wide)], g.at[s + 1], g_sem.at[s + 1, 0]))
    loads = []
    for k, (c, n) in enumerate(chunks):
        loads.append(
            [
                pltpu.make_async_copy(src.at[pl.ds(c, n)], w.at[pl.ds(c, n), pl.ds(i * wide, wide)], w_sem.at[k, i])
                for i, src in enumerate((w0, w1, w2, w3, w4, w5, w6, w7))
            ]
        )
    seconds = [pltpu.make_async_copy(own, gate.at[0], g_sem.at[0, NY]), pltpu.make_async_copy(proj, p, g_sem.at[1, NY])]
    for s, got in enumerate((x1, x2, x3)):
        seconds.append(pltpu.make_async_copy(got.at[:, pl.ds(0, hid)], gate.at[s + 1], g_sem.at[s + 1, 1]))
    for c in loads[0] + firsts + loads[1] + seconds:
        c.start()
    for load in loads[2:]:
        for c in load:
            c.start()
    for c in firsts:
        c.wait()
    grads = g[...].reshape(nx * tok, NY * wide)
    total = [None] * nx
    for k, (c, n) in enumerate(chunks):
        for cp in loads[k]:
            cp.wait()
        gh = dot_nt(grads, w[c : c + n, :])
        if k == 0:
            for cp in seconds:
                cp.wait()
        gu = gh * silu(gate[:, :, c : c + n].reshape(nx * tok, n).astype(F32))
        hi = gu.astype(BF16)
        lo = (gu - hi.astype(F32)).astype(BF16)
        ps = p[:, c : c + n]
        for s in range(nx):
            rows = slice(s * tok, (s + 1) * tok)
            part = dot_nt(ps, hi[rows]) + dot_nt(ps, lo[rows])
            total[s] = part if k == 0 else total[s] + part
    for s in range(nx):
        to = lax.rem(x - s + nx, nx)
        for b in range(NB):
            out[to, b] = total[s][b * per : (b + 1) * per, :]


def main(grad, own, got, shards, proj):
    tok = grad.shape[0]
    hid, wide = shards[0].shape
    per = proj.shape[0] // NB
    n_chunk = -(-hid // CHUNK)
    return pl.pallas_call(
        main_kernel,
        out_shape=jax.ShapeDtypeStruct((NX, NB, per, tok), F32),
        in_specs=[HBM] * 14,
        out_specs=VMEM,
        scratch_shapes=[
            pltpu.VMEM((NX, tok, NY * wide), BF16),
            pltpu.VMEM((NX, tok, hid), BF16),
            pltpu.VMEM((hid, NY * wide), BF16),
            pltpu.VMEM(proj.shape, BF16),
            pltpu.SemaphoreType.DMA((NX, NY + 1)),
            pltpu.SemaphoreType.DMA((n_chunk, NY)),
        ],
        compiler_params=pltpu.CompilerParams(vmem_limit_bytes=32 << 20),
        cost_estimate=pl.CostEstimate(
            flops=16 * NX * tok * hid * (NY * wide + 128), bytes_accessed=9_000_000, transcendentals=NX * tok * hid
        ),
        name="main",
    )(grad, own, *got, *shards, proj)


def score(left, right, which, out):
    picked = jnp.concatenate([jnp.where(which == e, left, 0.0) for e in range(2)], axis=0)
    res = jnp.dot(picked, right, precision=lax.Precision.HIGHEST, preferred_element_type=F32)
    per, width = left.shape[0], right.shape[1]
    for e in range(2):
        for k in range(per):
            out[e : e + 1, k * width : (k + 1) * width] = res[e * per + k : e * per + k + 1, :]


def settle_kernel(got, ids, down, side):
    tok = ids.shape[1]
    total = got[0].astype(F32)
    for b in range(1, NB):
        total = total + got[b].astype(F32)
    width = side.shape[1]
    per = down.shape[1] // width
    hid_side = total[tok : tok + per, 0:tok] + total[tok + per : tok + 2 * per, 0:tok]
    score(hid_side, total[0:tok, 0:width], ids[...], down)
    side[...] = total[0:tok, width:]


def settle(got, ids, per):
    tok, width = ids.shape[1], got.shape[2] // 2
    return pl.pallas_call(
        settle_kernel,
        out_shape=[jax.ShapeDtypeStruct((2, per * width), F32), jax.ShapeDtypeStruct((tok, width), F32)],
        in_specs=[VMEM, VMEM],
        out_specs=[VMEM, VMEM],
        name="settle",
    )(got, ids)


def finish_kernel(got, side, ids, up):
    parts = [got[b] for b in range(got.shape[0])]
    while len(parts) > 1:
        parts = [parts[i] + parts[i + 1] for i in range(0, len(parts), 2)]
    score(parts[0], side[...], ids[...], up)


def finish(got, side, ids):
    return pl.pallas_call(
        finish_kernel,
        out_shape=jax.ShapeDtypeStruct((2, got.shape[1] * side.shape[1]), F32),
        in_specs=[VMEM] * 3,
        out_specs=VMEM,
        name="finish",
    )(got, side, ids)


def on_device(out_grad, layer_input, gate_pre, up_pre, down_weight, proj_hidden, proj_model, example_ids):
    hproj = proj_hidden.T
    up1 = lax.ppermute(down_weight, "y", turn(NY, 1))
    dn1 = lax.ppermute(down_weight, "y", turn(NY, -1))
    p1, p2, p3, early = prepare(out_grad, gate_pre, up_pre, layer_input, proj_model, hproj, down_weight.shape[1])
    up1, dn1, early = lax.optimization_barrier((up1, dn1, early))
    x1, x2, x3 = [lax.ppermute(p, "x", turn(NX, s + 1)) for s, p in enumerate((p1, p2, p3))]
    up2 = lax.ppermute(up1, "y", turn(NY, 1))
    dn2 = lax.ppermute(dn1, "y", turn(NY, -1))
    got = lax.all_to_all(early, ZC, 0, 0)
    up3 = lax.ppermute(up2, "y", turn(NY, 1))
    dn3 = lax.ppermute(dn2, "y", turn(NY, -1))
    up3, dn3, x1, x3 = lax.optimization_barrier((up3, dn3, x1, x3))
    w4 = lax.ppermute(up3, "y", turn(NY, 1))
    x2, w4 = lax.optimization_barrier((x2, w4))
    up_part = main(out_grad, gate_pre, (x1, x2, x3), (down_weight, up1, up2, up3, w4, dn3, dn2, dn1), hproj)
    up_part, got = lax.optimization_barrier((up_part, got))
    up_side = lax.all_to_all(up_part.reshape((NX * NB,) + up_part.shape[2:]), ("x",) + ZC, 0, 0)
    down_scores, side = settle(got, example_ids, up_part.shape[2])
    return down_scores, finish(up_side, side, example_ids)


def solution(mesh):
    fine = Mesh(mesh.devices.reshape(NY, NX, NZ, NC), ("y", "x", "z", "core"))
    yx = ("y", "x")
    in_specs = (P(yx, None), P(yx, ZC), P(yx, ZC), P(yx, ZC), P(ZC, yx), P(ZC, None), P(ZC, None), P(yx, None))
    out_specs = (P(yx, ZC), P(yx, ZC))
    return jax.shard_map(on_device, mesh=fine, in_specs=in_specs, out_specs=out_specs, check_vma=False)
```

```python
import jax
import jax.numpy as jnp
from jax import lax
from jax.experimental import pallas as pl
from jax.experimental.pallas import tpu as pltpu
from jax.sharding import Mesh
from jax.sharding import PartitionSpec as P

NY, NX, NZ, NC = 8, 4, 8, 2
NB = NZ * NC
FAR = NY // 2
EXTRA = 16
ZC = ("z", "core")
BF16, F32 = jnp.bfloat16, jnp.float32
HBM = pl.BlockSpec(memory_space=pltpu.HBM)
VMEM = pl.BlockSpec(memory_space=pltpu.VMEM)
WIDE = pltpu.CompilerParams(vmem_limit_bytes=60 << 20)


def turn(n, step):
    return [(i, (i + step) % n) for i in range(n)]


def dot_nt(a, b, **kw):
    return lax.dot_general(a, b, (((1,), (1,)), ((), ())), preferred_element_type=F32, **kw)


def silu(v):
    return v / (1.0 + jnp.exp(-v))


def columns(y, back, x, wide):
    return pl.multiple_of((lax.rem(y - back + NY, NY) * NX + x) * wide, wide)


def here():
    return lax.axis_index("y"), lax.axis_index("x"), lax.axis_index("z") * NC + lax.axis_index("core")


def prepare_kernel(grad, gate, up, inp, model, hproj, p1, p2, p3, early, buf, gate_v, up_v, inp_v, gcols, model_v, hproj_v, in_sem, out_sem, side_sem):
    outs = (p1, p2, p3)
    tok, hid = gate.shape
    wide = (p1.shape[1] - hid) // NY
    feat = inp.shape[1]
    y, x, blk = here()
    fills, sends = [], []
    for s, out in enumerate(outs):
        at = lax.rem(x + s + 1, NX)
        fill = [pltpu.make_async_copy(gate, buf.at[s, :, pl.ds(0, hid)], in_sem.at[s, NY])]
        for i in range(NY):
            fill.append(
                pltpu.make_async_copy(
                    grad.at[:, pl.ds(columns(y, i, at, wide), wide)],
                    buf.at[s, :, pl.ds(hid + i * wide, wide)],
                    in_sem.at[s, i],
                )
            )
        fills.append(fill)
        sends.append(pltpu.make_async_copy(buf.at[s], out, out_sem.at[s]))
        for c in fill:
            c.start()
    loads = [
        pltpu.make_async_copy(gate, gate_v, side_sem.at[0]),
        pltpu.make_async_copy(up, up_v, side_sem.at[1]),
        pltpu.make_async_copy(inp, inp_v, side_sem.at[2]),
        pltpu.make_async_copy(grad.at[:, pl.ds(pl.multiple_of(blk * feat, feat), feat)], gcols, side_sem.at[3]),
        pltpu.make_async_copy(model, model_v, side_sem.at[4]),
        pltpu.make_async_copy(hproj, hproj_v, side_sem.at[5]),
    ]
    for c in loads:
        c.start()
    for fill, send in zip(fills, sends):
        for c in fill:
            c.wait()
        send.start()
    for c in loads:
        c.wait()
    hidden = (silu(gate_v[...].astype(F32)) * up_v[...].astype(F32)).astype(BF16)
    hid_side = dot_nt(hproj_v[...], hidden)
    high = hid_side.astype(BF16).astype(F32)
    low = hid_side - high
    m = model_v[...]
    side = jnp.concatenate(
        [jnp.dot(v[...], m, preferred_element_type=F32) for v in (gcols, inp_v)], axis=1
    ).astype(BF16)
    width = side.shape[1]
    per = hproj.shape[0] // NB
    half = tok // NC
    for b in range(NB):
        early[b, 0:half, :] = side[(b % NC) * half : (b % NC + 1) * half]
        rows = jnp.concatenate(
            [high[b * per : (b + 1) * per], low[b * per : (b + 1) * per], jnp.zeros((EXTRA - 2 * per, tok), F32)], axis=0
        )
        early[b, half : half + EXTRA, :] = jnp.concatenate(
            [rows, jnp.zeros((EXTRA, width - tok), F32)], axis=1
        ).astype(BF16)
    for c in sends:
        c.wait()


def prepare(grad, gate, up, inp, model, hproj, wide):
    tok, hid = gate.shape
    feat = inp.shape[1]
    out = jax.ShapeDtypeStruct((tok, hid + NY * wide), BF16)
    return pl.pallas_call(
        prepare_kernel,
        out_shape=[out] * 3 + [jax.ShapeDtypeStruct((NB, tok // NC + EXTRA, 2 * model.shape[1]), BF16)],
        in_specs=[HBM] * 6,
        out_specs=[HBM] * 3 + [VMEM],
        scratch_shapes=[
            pltpu.VMEM((NX - 1, tok, hid + NY * wide), BF16),
            pltpu.VMEM((tok, hid), BF16),
            pltpu.VMEM((tok, hid), BF16),
            pltpu.VMEM((tok, feat), BF16),
            pltpu.VMEM((tok, feat), BF16),
            pltpu.VMEM(model.shape, BF16),
            pltpu.VMEM(hproj.shape, BF16),
            pltpu.SemaphoreType.DMA((NX - 1, NY + 1)),
            pltpu.SemaphoreType.DMA((NX - 1,)),
            pltpu.SemaphoreType.DMA((6,)),
        ],
        compiler_params=WIDE,
        cost_estimate=pl.CostEstimate(flops=80_000_000, bytes_accessed=8_000_000, transcendentals=tok * hid),
        name="prepare",
    )(grad, gate, up, inp, model, hproj)


def main_kernel(grad, own, x1, x2, x3, w0, w1, w2, w3, w4, w5, w6, w7, proj, out, g, gate, w, p, g_sem, w_sem):
    y, x, _ = here()
    nx, tok, hid = gate.shape
    wide = w0.shape[1]
    per = proj.shape[0] // NB
    firsts = []
    for i in range(NY):
        firsts.append(
            pltpu.make_async_copy(
                grad.at[:, pl.ds(columns(y, i, x, wide), wide)], g.at[0, :, pl.ds(i * wide, wide)], g_sem.at[0, i]
            )
        )
    for s, got in enumerate((x1, x2, x3)):
        firsts.append(pltpu.make_async_copy(got.at[:, pl.ds(hid, NY * wide)], g.at[s + 1], g_sem.at[s + 1, 0]))
    for i, src in enumerate((w0, w1, w2, w3, w4, w5, w6, w7)):
        firsts.append(pltpu.make_async_copy(src, w.at[:, pl.ds(i * wide, wide)], w_sem.at[i]))
    seconds = [pltpu.make_async_copy(own, gate.at[0], g_sem.at[0, NY]), pltpu.make_async_copy(proj, p, g_sem.at[1, NY])]
    for s, got in enumerate((x1, x2, x3)):
        seconds.append(pltpu.make_async_copy(got.at[:, pl.ds(0, hid)], gate.at[s + 1], g_sem.at[s + 1, 1]))
    for c in firsts + seconds:
        c.start()
    for c in firsts:
        c.wait()
    gh = dot_nt(g[...].reshape(nx * tok, NY * wide), w[...])
    for c in seconds:
        c.wait()
    gu = gh * silu(gate[...].reshape(nx * tok, hid).astype(F32))
    hi = gu.astype(BF16)
    lo = (gu - hi.astype(F32)).astype(BF16)
    for s in range(nx):
        rows = slice(s * tok, (s + 1) * tok)
        total = dot_nt(p[...], hi[rows]) + dot_nt(p[...], lo[rows])
        to = lax.rem(x - s + nx, nx)
        for b in range(NB):
            out[to, b] = total[b * per : (b + 1) * per, :]


def main(grad, own, got, shards, proj):
    tok = grad.shape[0]
    hid, wide = shards[0].shape
    per = proj.shape[0] // NB
    return pl.pallas_call(
        main_kernel,
        out_shape=jax.ShapeDtypeStruct((NX, NB, per, tok), F32),
        in_specs=[HBM] * 14,
        out_specs=VMEM,
        scratch_shapes=[
            pltpu.VMEM((NX, tok, NY * wide), BF16),
            pltpu.VMEM((NX, tok, hid), BF16),
            pltpu.VMEM((hid, NY * wide), BF16),
            pltpu.VMEM(proj.shape, BF16),
            pltpu.SemaphoreType.DMA((NX, NY + 1)),
            pltpu.SemaphoreType.DMA((NY,)),
        ],
        compiler_params=pltpu.CompilerParams(vmem_limit_bytes=32 << 20),
        cost_estimate=pl.CostEstimate(
            flops=7 * NX * tok * hid * (NY * wide + 128), bytes_accessed=9_000_000, transcendentals=NX * tok * hid
        ),
        name="main",
    )(grad, own, *got, *shards, proj)


def score(left, right, which, out):
    picked = jnp.concatenate([jnp.where(which == e, left, 0.0) for e in range(2)], axis=0)
    res = jnp.dot(picked, right, precision=lax.Precision.HIGHEST, preferred_element_type=F32)
    per, width = left.shape[0], right.shape[1]
    for e in range(2):
        for k in range(per):
            out[e : e + 1, k * width : (k + 1) * width] = res[e * per + k : e * per + k + 1, :]


def settle_kernel(got, side, hid_side):
    total = got[0].astype(F32)
    for b in range(1, NB):
        total = total + got[b].astype(F32)
    half = side.shape[0]
    per, tok = hid_side.shape
    side[...] = total[:half]
    hid_side[...] = total[half : half + per, 0:tok] + total[half + per : half + 2 * per, 0:tok]


def settle(got, per):
    _, rows, width = got.shape
    half = rows - EXTRA
    return pl.pallas_call(
        settle_kernel,
        out_shape=[jax.ShapeDtypeStruct((half, width), F32), jax.ShapeDtypeStruct((per, half * NC), F32)],
        in_specs=[VMEM],
        out_specs=[VMEM, VMEM],
        name="settle",
    )(got)


def finish_kernel(got, hid_side, mine, other, ids, down, up):
    first = lax.axis_index("core") == 0
    side = jnp.concatenate(
        [jnp.where(first, mine[...], other[...]), jnp.where(first, other[...], mine[...])], axis=0
    )
    width = side.shape[1] // 2
    parts = [got[b] for b in range(got.shape[0])]
    while len(parts) > 1:
        parts = [parts[i] + parts[i + 1] for i in range(0, len(parts), 2)]
    score(hid_side[...], side[:, :width], ids[...], down)
    score(parts[0], side[:, width:], ids[...], up)


def finish(got, hid_side, mine, other, ids):
    out = jax.ShapeDtypeStruct((2, got.shape[1] * mine.shape[1] // 2), F32)
    return pl.pallas_call(
        finish_kernel, out_shape=[out, out], in_specs=[VMEM] * 5, out_specs=[VMEM, VMEM], name="finish"
    )(got, hid_side, mine, other, ids)


def on_device(out_grad, layer_input, gate_pre, up_pre, down_weight, proj_hidden, proj_model, example_ids):
    hproj = proj_hidden.T
    up1 = lax.ppermute(down_weight, "y", turn(NY, 1))
    dn1 = lax.ppermute(down_weight, "y", turn(NY, -1))
    p1, p2, p3, early = prepare(out_grad, gate_pre, up_pre, layer_input, proj_model, hproj, down_weight.shape[1])
    up1, dn1, early = lax.optimization_barrier((up1, dn1, early))
    x1, x2, x3 = [lax.ppermute(p, "x", turn(NX, s + 1)) for s, p in enumerate((p1, p2, p3))]
    up2 = lax.ppermute(up1, "y", turn(NY, 1))
    dn2 = lax.ppermute(dn1, "y", turn(NY, -1))
    got = lax.all_to_all(early, ZC, 0, 0)
    up3 = lax.ppermute(up2, "y", turn(NY, 1))
    dn3 = lax.ppermute(dn2, "y", turn(NY, -1))
    up3, dn3, x1 = lax.optimization_barrier((up3, dn3, x1))
    w4 = lax.ppermute(up3, "y", turn(NY, 1))
    x2, x3, w4 = lax.optimization_barrier((x2, x3, w4))
    up_part = main(out_grad, gate_pre, (x1, x2, x3), (down_weight, up1, up2, up3, w4, dn3, dn2, dn1), hproj)
    up_part, got = lax.optimization_barrier((up_part, got))
    up_side = lax.all_to_all(up_part.reshape((NX * NB,) + up_part.shape[2:]), ("x",) + ZC, 0, 0)
    mine, hid_side = settle(got, up_part.shape[2])
    other = lax.ppermute(mine, "core", turn(NC, 1))
    return tuple(finish(up_side, hid_side, mine, other, example_ids))


def solution(mesh):
    fine = Mesh(mesh.devices.reshape(NY, NX, NZ, NC), ("y", "x", "z", "core"))
    yx = ("y", "x")
    in_specs = (P(yx, None), P(yx, ZC), P(yx, ZC), P(yx, ZC), P(ZC, yx), P(ZC, None), P(ZC, None), P(yx, None))
    out_specs = (P(yx, ZC), P(yx, ZC))
    return jax.shard_map(on_device, mesh=fine, in_specs=in_specs, out_specs=out_specs, check_vma=False)
```

```python
import jax
import jax.numpy as jnp
from jax import lax
from jax.experimental import pallas as pl
from jax.experimental.pallas import tpu as pltpu
from jax.sharding import Mesh
from jax.sharding import PartitionSpec as P

NY, NX, NZ, NC = 8, 4, 8, 2
NB = NZ * NC
HALF = NY // NC
EXTRA = 16
ZC = ("z", "core")
BF16, F32 = jnp.bfloat16, jnp.float32
HBM = pl.BlockSpec(memory_space=pltpu.HBM)
VMEM = pl.BlockSpec(memory_space=pltpu.VMEM)
WIDE = pltpu.CompilerParams(vmem_limit_bytes=60 << 20)


def turn(n, step):
    return [(i, (i + step) % n) for i in range(n)]


def dot_nt(a, b, **kw):
    return lax.dot_general(a, b, (((1,), (1,)), ((), ())), preferred_element_type=F32, **kw)


def silu(v):
    return v / (1.0 + jnp.exp(-v))


def columns(y, back, x, wide):
    return pl.multiple_of((lax.rem(y - back + NY, NY) * NX + x) * wide, wide)


def here():
    return lax.axis_index("y"), lax.axis_index("x"), lax.axis_index("z") * NC + lax.axis_index("core")


def prepare_kernel(grad, gate, up, inp, model, hproj, p1, p2, p3, early, buf, gate_v, up_v, inp_v, gcols, model_v, hproj_v, in_sem, out_sem, side_sem):
    outs = (p1, p2, p3)
    tok, hid = gate.shape
    wide = (p1.shape[1] - hid) // HALF
    core = lax.axis_index("core")
    feat = inp.shape[1]
    y, x, blk = here()
    fills, sends = [], []
    for s, out in enumerate(outs):
        at = lax.rem(x + s + 1, NX)
        fill = [pltpu.make_async_copy(gate, buf.at[s, :, pl.ds(0, hid)], in_sem.at[s, HALF])]
        for i in range(HALF):
            fill.append(
                pltpu.make_async_copy(
                    grad.at[:, pl.ds(columns(y, core * HALF + i, at, wide), wide)],
                    buf.at[s, :, pl.ds(hid + i * wide, wide)],
                    in_sem.at[s, i],
                )
            )
        fills.append(fill)
        sends.append(pltpu.make_async_copy(buf.at[s], out, out_sem.at[s]))
        for c in fill:
            c.start()
    loads = [
        pltpu.make_async_copy(gate, gate_v, side_sem.at[0]),
        pltpu.make_async_copy(up, up_v, side_sem.at[1]),
        pltpu.make_async_copy(inp, inp_v, side_sem.at[2]),
        pltpu.make_async_copy(grad.at[:, pl.ds(pl.multiple_of(blk * feat, feat), feat)], gcols, side_sem.at[3]),
        pltpu.make_async_copy(model, model_v, side_sem.at[4]),
        pltpu.make_async_copy(hproj, hproj_v, side_sem.at[5]),
    ]
    for c in loads:
        c.start()
    for fill, send in zip(fills, sends):
        for c in fill:
            c.wait()
        send.start()
    for c in loads:
        c.wait()
    hidden = (silu(gate_v[...].astype(F32)) * up_v[...].astype(F32)).astype(BF16)
    hid_side = dot_nt(hproj_v[...], hidden)
    high = hid_side.astype(BF16).astype(F32)
    low = hid_side - high
    m = model_v[...]
    side = jnp.concatenate(
        [jnp.dot(v[...], m, preferred_element_type=F32) for v in (gcols, inp_v)], axis=1
    ).astype(BF16)
    width = side.shape[1]
    per = hproj.shape[0] // NB
    half = tok // NC
    for b in range(NB):
        early[b, 0:half, :] = side[(b % NC) * half : (b % NC + 1) * half]
        rows = jnp.concatenate(
            [high[b * per : (b + 1) * per], low[b * per : (b + 1) * per], jnp.zeros((EXTRA - 2 * per, tok), F32)], axis=0
        )
        early[b, half : half + EXTRA, :] = jnp.concatenate(
            [rows, jnp.zeros((EXTRA, width - tok), F32)], axis=1
        ).astype(BF16)
    for c in sends:
        c.wait()


def prepare(grad, gate, up, inp, model, hproj, wide):
    tok, hid = gate.shape
    feat = inp.shape[1]
    out = jax.ShapeDtypeStruct((tok, hid + HALF * wide), BF16)
    return pl.pallas_call(
        prepare_kernel,
        out_shape=[out] * 3 + [jax.ShapeDtypeStruct((NB, tok // NC + EXTRA, 2 * model.shape[1]), BF16)],
        in_specs=[HBM] * 6,
        out_specs=[HBM] * 3 + [VMEM],
        scratch_shapes=[
            pltpu.VMEM((NX - 1, tok, hid + HALF * wide), BF16),
            pltpu.VMEM((tok, hid), BF16),
            pltpu.VMEM((tok, hid), BF16),
            pltpu.VMEM((tok, feat), BF16),
            pltpu.VMEM((tok, feat), BF16),
            pltpu.VMEM(model.shape, BF16),
            pltpu.VMEM(hproj.shape, BF16),
            pltpu.SemaphoreType.DMA((NX - 1, HALF + 1)),
            pltpu.SemaphoreType.DMA((NX - 1,)),
            pltpu.SemaphoreType.DMA((6,)),
        ],
        compiler_params=WIDE,
        cost_estimate=pl.CostEstimate(flops=80_000_000, bytes_accessed=8_000_000, transcendentals=tok * hid),
        name="prepare",
    )(grad, gate, up, inp, model, hproj)


def main_kernel(grad, own, x1, x2, x3, o1, o2, o3, w0, w1, w2, w3, w4, w5, w6, w7, proj, out, g, gate, w, p, g_sem, w_sem):
    y, x, _ = here()
    core = lax.axis_index("core")
    nx, tok, hid = gate.shape
    wide = w0.shape[1]
    n = HALF * wide
    near = pl.ds(pl.multiple_of(core * n, n), n)
    away = pl.ds(pl.multiple_of((1 - core) * n, n), n)
    per = proj.shape[0] // NB
    firsts = []
    for i in range(NY):
        firsts.append(
            pltpu.make_async_copy(
                grad.at[:, pl.ds(columns(y, i, x, wide), wide)], g.at[0, :, pl.ds(i * wide, wide)], g_sem.at[0, i]
            )
        )
    for s, (mine, other) in enumerate(((x1, o1), (x2, o2), (x3, o3))):
        firsts.append(pltpu.make_async_copy(mine.at[:, pl.ds(hid, n)], g.at[s + 1, :, near], g_sem.at[s + 1, 0]))
        firsts.append(pltpu.make_async_copy(other.at[:, pl.ds(hid, n)], g.at[s + 1, :, away], g_sem.at[s + 1, 1]))
    for i, src in enumerate((w0, w1, w2, w3, w4, w5, w6, w7)):
        firsts.append(pltpu.make_async_copy(src, w.at[:, pl.ds(i * wide, wide)], w_sem.at[i]))
    seconds = [pltpu.make_async_copy(own, gate.at[0], g_sem.at[0, NY]), pltpu.make_async_copy(proj, p, g_sem.at[1, NY])]
    for s, got in enumerate((x1, x2, x3)):
        seconds.append(pltpu.make_async_copy(got.at[:, pl.ds(0, hid)], gate.at[s + 1], g_sem.at[s + 1, 2]))
    for c in firsts + seconds:
        c.start()
    for c in firsts:
        c.wait()
    gh = dot_nt(g[...].reshape(nx * tok, NY * wide), w[...])
    for c in seconds:
        c.wait()
    gu = gh * silu(gate[...].reshape(nx * tok, hid).astype(F32))
    hi = gu.astype(BF16)
    lo = (gu - hi.astype(F32)).astype(BF16)
    for s in range(nx):
        rows = slice(s * tok, (s + 1) * tok)
        total = dot_nt(p[...], hi[rows]) + dot_nt(p[...], lo[rows])
        to = lax.rem(x - s + nx, nx)
        for b in range(NB):
            out[to, b] = total[b * per : (b + 1) * per, :]


def main(grad, own, got, swapped, shards, proj):
    tok = grad.shape[0]
    hid, wide = shards[0].shape
    per = proj.shape[0] // NB
    return pl.pallas_call(
        main_kernel,
        out_shape=jax.ShapeDtypeStruct((NX, NB, per, tok), F32),
        in_specs=[HBM] * 17,
        out_specs=VMEM,
        scratch_shapes=[
            pltpu.VMEM((NX, tok, NY * wide), BF16),
            pltpu.VMEM((NX, tok, hid), BF16),
            pltpu.VMEM((hid, NY * wide), BF16),
            pltpu.VMEM(proj.shape, BF16),
            pltpu.SemaphoreType.DMA((NX, NY + 1)),
            pltpu.SemaphoreType.DMA((NY,)),
        ],
        compiler_params=pltpu.CompilerParams(vmem_limit_bytes=50 << 20),
        cost_estimate=pl.CostEstimate(
            flops=4 * NX * tok * hid * (NY * wide + 128), bytes_accessed=9_000_000, transcendentals=NX * tok * hid
        ),
        name="main",
    )(grad, own, *got, *swapped, *shards, proj)


def score(left, right, which, out):
    picked = jnp.concatenate([jnp.where(which == e, left, 0.0) for e in range(2)], axis=0)
    res = jnp.dot(picked, right, precision=lax.Precision.HIGHEST, preferred_element_type=F32)
    per, width = left.shape[0], right.shape[1]
    for e in range(2):
        for k in range(per):
            out[e : e + 1, k * width : (k + 1) * width] = res[e * per + k : e * per + k + 1, :]


def settle_kernel(got, side, hid_side):
    total = got[0].astype(F32)
    for b in range(1, NB):
        total = total + got[b].astype(F32)
    half = side.shape[0]
    per, tok = hid_side.shape
    side[...] = total[:half]
    hid_side[...] = total[half : half + per, 0:tok] + total[half + per : half + 2 * per, 0:tok]


def settle(got, per):
    _, rows, width = got.shape
    half = rows - EXTRA
    return pl.pallas_call(
        settle_kernel,
        out_shape=[jax.ShapeDtypeStruct((half, width), F32), jax.ShapeDtypeStruct((per, half * NC), F32)],
        in_specs=[VMEM],
        out_specs=[VMEM, VMEM],
        name="settle",
    )(got)


def finish_kernel(got, hid_side, mine, other, ids, down, up):
    first = lax.axis_index("core") == 0
    side = jnp.concatenate(
        [jnp.where(first, mine[...], other[...]), jnp.where(first, other[...], mine[...])], axis=0
    )
    width = side.shape[1] // 2
    parts = [got[b] for b in range(got.shape[0])]
    while len(parts) > 1:
        parts = [parts[i] + parts[i + 1] for i in range(0, len(parts), 2)]
    score(hid_side[...], side[:, :width], ids[...], down)
    score(parts[0], side[:, width:], ids[...], up)


def finish(got, hid_side, mine, other, ids):
    out = jax.ShapeDtypeStruct((2, got.shape[1] * mine.shape[1] // 2), F32)
    return pl.pallas_call(
        finish_kernel, out_shape=[out, out], in_specs=[VMEM] * 5, out_specs=[VMEM, VMEM], name="finish"
    )(got, hid_side, mine, other, ids)


def on_device(out_grad, layer_input, gate_pre, up_pre, down_weight, proj_hidden, proj_model, example_ids):
    hproj = proj_hidden.T
    up1 = lax.ppermute(down_weight, "y", turn(NY, 1))
    dn1 = lax.ppermute(down_weight, "y", turn(NY, -1))
    p1, p2, p3, early = prepare(out_grad, gate_pre, up_pre, layer_input, proj_model, hproj, down_weight.shape[1])
    up1, dn1, early = lax.optimization_barrier((up1, dn1, early))
    x1, x2, x3 = [lax.ppermute(p, "x", turn(NX, s + 1)) for s, p in enumerate((p1, p2, p3))]
    up2 = lax.ppermute(up1, "y", turn(NY, 1))
    dn2 = lax.ppermute(dn1, "y", turn(NY, -1))
    got = lax.all_to_all(early, ZC, 0, 0)
    up2, dn2, x1 = lax.optimization_barrier((up2, dn2, x1))
    up3 = lax.ppermute(up2, "y", turn(NY, 1))
    dn3 = lax.ppermute(dn2, "y", turn(NY, -1))
    up3, dn3, x3 = lax.optimization_barrier((up3, dn3, x3))
    w4 = lax.ppermute(up3, "y", turn(NY, 1))
    o1, o2, o3 = [lax.ppermute(v, "core", turn(NC, 1)) for v in (x1, x2, x3)]
    o1, o2, o3, w4 = lax.optimization_barrier((o1, o2, o3, w4))
    up_part = main(out_grad, gate_pre, (x1, x2, x3), (o1, o2, o3), (down_weight, up1, up2, up3, w4, dn3, dn2, dn1), hproj)
    up_part, got = lax.optimization_barrier((up_part, got))
    up_side = lax.all_to_all(up_part.reshape((NX * NB,) + up_part.shape[2:]), ("x",) + ZC, 0, 0)
    mine, hid_side = settle(got, up_part.shape[2])
    other = lax.ppermute(mine, "core", turn(NC, 1))
    return tuple(finish(up_side, hid_side, mine, other, example_ids))


def solution(mesh):
    fine = Mesh(mesh.devices.reshape(NY, NX, NZ, NC), ("y", "x", "z", "core"))
    yx = ("y", "x")
    in_specs = (P(yx, None), P(yx, ZC), P(yx, ZC), P(yx, ZC), P(ZC, yx), P(ZC, None), P(ZC, None), P(yx, None))
    out_specs = (P(yx, ZC), P(yx, ZC))
    return jax.shard_map(on_device, mesh=fine, in_specs=in_specs, out_specs=out_specs, check_vma=False)
```

```python
import jax
import jax.numpy as jnp
from jax import lax
from jax.experimental import pallas as pl
from jax.experimental.pallas import tpu as pltpu
from jax.sharding import Mesh
from jax.sharding import PartitionSpec as P

NY, NX, NZ, NC = 8, 4, 8, 2
NB = NZ * NC
HALF = NY // NC
EXTRA = 16
ZC = ("z", "core")
BF16, F32 = jnp.bfloat16, jnp.float32
HBM = pl.BlockSpec(memory_space=pltpu.HBM)
VMEM = pl.BlockSpec(memory_space=pltpu.VMEM)
WIDE = pltpu.CompilerParams(vmem_limit_bytes=60 << 20)


def turn(n, step):
    return [(i, (i + step) % n) for i in range(n)]


def dot_nt(a, b, **kw):
    return lax.dot_general(a, b, (((1,), (1,)), ((), ())), preferred_element_type=F32, **kw)


def silu(v):
    return v / (1.0 + jnp.exp(-v))


def columns(y, back, x, wide):
    return pl.multiple_of((lax.rem(y - back + NY, NY) * NX + x) * wide, wide)


def here():
    return lax.axis_index("y"), lax.axis_index("x"), lax.axis_index("z") * NC + lax.axis_index("core")


def prepare_kernel(grad, gate, up, inp, model, hproj, p1, p2, p3, early, buf, gate_v, up_v, inp_v, gcols, model_v, hproj_v, in_sem, out_sem, side_sem):
    tok, hid = gate.shape
    feat = inp.shape[1]
    y, x, blk = here()
    core = lax.axis_index("core")
    wide = (p1.shape[1] - hid) // NY
    fills, sends = [], []
    for s, out in ((2, p2), (1, p1), (3, p3)):
        at = lax.rem(x + s, NX)
        size = out.shape[1]
        part = (size - hid) // wide
        first = core * HALF if part < NY else 0
        fill = [pltpu.make_async_copy(gate, buf.at[s - 1, :, pl.ds(0, hid)], in_sem.at[s - 1, NY])]
        for i in range(part):
            fill.append(
                pltpu.make_async_copy(
                    grad.at[:, pl.ds(columns(y, first + i, at, wide), wide)],
                    buf.at[s - 1, :, pl.ds(hid + i * wide, wide)],
                    in_sem.at[s - 1, i],
                )
            )
        fills.append(fill)
        sends.append(pltpu.make_async_copy(buf.at[s - 1, :, pl.ds(0, size)], out, out_sem.at[s - 1]))
        for c in fill:
            c.start()
    loads = [
        pltpu.make_async_copy(gate, gate_v, side_sem.at[0]),
        pltpu.make_async_copy(up, up_v, side_sem.at[1]),
        pltpu.make_async_copy(inp, inp_v, side_sem.at[2]),
        pltpu.make_async_copy(grad.at[:, pl.ds(pl.multiple_of(blk * feat, feat), feat)], gcols, side_sem.at[3]),
        pltpu.make_async_copy(model, model_v, side_sem.at[4]),
        pltpu.make_async_copy(hproj, hproj_v, side_sem.at[5]),
    ]
    for c in loads:
        c.start()
    for fill, send in zip(fills, sends):
        for c in fill:
            c.wait()
        send.start()
    for c in loads:
        c.wait()
    hidden = (silu(gate_v[...].astype(F32)) * up_v[...].astype(F32)).astype(BF16)
    hid_side = dot_nt(hproj_v[...], hidden)
    high = hid_side.astype(BF16).astype(F32)
    low = hid_side - high
    m = model_v[...]
    side = jnp.concatenate(
        [jnp.dot(v[...], m, preferred_element_type=F32) for v in (gcols, inp_v)], axis=1
    ).astype(BF16)
    width = side.shape[1]
    per = hproj.shape[0] // NB
    half = tok // NC
    for b in range(NB):
        early[b, 0:half, :] = side[(b % NC) * half : (b % NC + 1) * half]
        rows = jnp.concatenate(
            [high[b * per : (b + 1) * per], low[b * per : (b + 1) * per], jnp.zeros((EXTRA - 2 * per, tok), F32)], axis=0
        )
        early[b, half : half + EXTRA, :] = jnp.concatenate(
            [rows, jnp.zeros((EXTRA, width - tok), F32)], axis=1
        ).astype(BF16)
    for c in sends:
        c.wait()


def prepare(grad, gate, up, inp, model, hproj, wide):
    tok, hid = gate.shape
    feat = inp.shape[1]
    full, part = [jax.ShapeDtypeStruct((tok, hid + n * wide), BF16) for n in (NY, HALF)]
    return pl.pallas_call(
        prepare_kernel,
        out_shape=[full, part, full] + [jax.ShapeDtypeStruct((NB, tok // NC + EXTRA, 2 * model.shape[1]), BF16)],
        in_specs=[HBM] * 6,
        out_specs=[HBM] * 3 + [VMEM],
        scratch_shapes=[
            pltpu.VMEM((NX - 1, tok, hid + NY * wide), BF16),
            pltpu.VMEM((tok, hid), BF16),
            pltpu.VMEM((tok, hid), BF16),
            pltpu.VMEM((tok, feat), BF16),
            pltpu.VMEM((tok, feat), BF16),
            pltpu.VMEM(model.shape, BF16),
            pltpu.VMEM(hproj.shape, BF16),
            pltpu.SemaphoreType.DMA((NX - 1, NY + 1)),
            pltpu.SemaphoreType.DMA((NX - 1,)),
            pltpu.SemaphoreType.DMA((6,)),
        ],
        compiler_params=WIDE,
        cost_estimate=pl.CostEstimate(flops=80_000_000, bytes_accessed=8_000_000, transcendentals=tok * hid),
        name="prepare",
    )(grad, gate, up, inp, model, hproj)


def main_kernel(grad, own, x1, x2, x3, o2, w0, w1, w2, w3, w4, w5, w6, w7, proj, out, g, gate, w, p, g_sem, w_sem):
    y, x, _ = here()
    core = lax.axis_index("core")
    nx, tok, hid = gate.shape
    wide = w0.shape[1]
    n = HALF * wide
    near = pl.ds(pl.multiple_of(core * n, n), n)
    away = pl.ds(pl.multiple_of((1 - core) * n, n), n)
    per = proj.shape[0] // NB
    firsts = []
    for i in range(NY):
        firsts.append(
            pltpu.make_async_copy(
                grad.at[:, pl.ds(columns(y, i, x, wide), wide)], g.at[0, :, pl.ds(i * wide, wide)], g_sem.at[0, i]
            )
        )
    for s, got in ((1, x1), (3, x3)):
        firsts.append(pltpu.make_async_copy(got.at[:, pl.ds(hid, NY * wide)], g.at[s], g_sem.at[s, 0]))
    firsts.append(pltpu.make_async_copy(x2.at[:, pl.ds(hid, n)], g.at[2, :, near], g_sem.at[2, 0]))
    firsts.append(pltpu.make_async_copy(o2.at[:, pl.ds(hid, n)], g.at[2, :, away], g_sem.at[2, 1]))
    for i, src in enumerate((w0, w1, w2, w3, w4, w5, w6, w7)):
        firsts.append(pltpu.make_async_copy(src, w.at[:, pl.ds(i * wide, wide)], w_sem.at[i]))
    seconds = [pltpu.make_async_copy(own, gate.at[0], g_sem.at[0, NY]), pltpu.make_async_copy(proj, p, g_sem.at[1, NY])]
    for s, got in enumerate((x1, x2, x3)):
        seconds.append(pltpu.make_async_copy(got.at[:, pl.ds(0, hid)], gate.at[s + 1], g_sem.at[s + 1, 2]))
    for c in firsts + seconds:
        c.start()
    for c in firsts:
        c.wait()
    gh = dot_nt(g[...].reshape(nx * tok, NY * wide), w[...])
    for c in seconds:
        c.wait()
    gu = gh * silu(gate[...].reshape(nx * tok, hid).astype(F32))
    hi = gu.astype(BF16)
    lo = (gu - hi.astype(F32)).astype(BF16)
    for s in range(nx):
        rows = slice(s * tok, (s + 1) * tok)
        total = dot_nt(p[...], hi[rows]) + dot_nt(p[...], lo[rows])
        to = lax.rem(x - s + nx, nx)
        for b in range(NB):
            out[to, b] = total[b * per : (b + 1) * per, :]


def main(grad, own, got, shards, proj):
    tok = grad.shape[0]
    hid, wide = shards[0].shape
    per = proj.shape[0] // NB
    return pl.pallas_call(
        main_kernel,
        out_shape=jax.ShapeDtypeStruct((NX, NB, per, tok), F32),
        in_specs=[HBM] * 15,
        out_specs=VMEM,
        scratch_shapes=[
            pltpu.VMEM((NX, tok, NY * wide), BF16),
            pltpu.VMEM((NX, tok, hid), BF16),
            pltpu.VMEM((hid, NY * wide), BF16),
            pltpu.VMEM(proj.shape, BF16),
            pltpu.SemaphoreType.DMA((NX, NY + 1)),
            pltpu.SemaphoreType.DMA((NY,)),
        ],
        compiler_params=pltpu.CompilerParams(vmem_limit_bytes=50 << 20),
        cost_estimate=pl.CostEstimate(
            flops=8 * NX * tok * hid * (NY * wide + 128), bytes_accessed=9_000_000, transcendentals=NX * tok * hid
        ),
        name="main",
    )(grad, own, *got, *shards, proj)


def score(left, right, which, out):
    picked = jnp.concatenate([jnp.where(which == e, left, 0.0) for e in range(2)], axis=0)
    res = jnp.dot(picked, right, precision=lax.Precision.HIGHEST, preferred_element_type=F32)
    per, width = left.shape[0], right.shape[1]
    for e in range(2):
        for k in range(per):
            out[e : e + 1, k * width : (k + 1) * width] = res[e * per + k : e * per + k + 1, :]


def settle_kernel(got, side, hid_side):
    total = got[0].astype(F32)
    for b in range(1, NB):
        total = total + got[b].astype(F32)
    half = side.shape[0]
    per, tok = hid_side.shape
    side[...] = total[:half]
    hid_side[...] = total[half : half + per, 0:tok] + total[half + per : half + 2 * per, 0:tok]


def settle(got, per):
    _, rows, width = got.shape
    half = rows - EXTRA
    return pl.pallas_call(
        settle_kernel,
        out_shape=[jax.ShapeDtypeStruct((half, width), F32), jax.ShapeDtypeStruct((per, half * NC), F32)],
        in_specs=[VMEM],
        out_specs=[VMEM, VMEM],
        name="settle",
    )(got)


def finish_kernel(got, hid_side, mine, other, ids, down, up):
    first = lax.axis_index("core") == 0
    side = jnp.concatenate(
        [jnp.where(first, mine[...], other[...]), jnp.where(first, other[...], mine[...])], axis=0
    )
    width = side.shape[1] // 2
    parts = [got[b] for b in range(got.shape[0])]
    while len(parts) > 1:
        parts = [parts[i] + parts[i + 1] for i in range(0, len(parts), 2)]
    score(hid_side[...], side[:, :width], ids[...], down)
    score(parts[0], side[:, width:], ids[...], up)


def finish(got, hid_side, mine, other, ids):
    out = jax.ShapeDtypeStruct((2, got.shape[1] * mine.shape[1] // 2), F32)
    return pl.pallas_call(
        finish_kernel, out_shape=[out, out], in_specs=[VMEM] * 5, out_specs=[VMEM, VMEM], name="finish"
    )(got, hid_side, mine, other, ids)


def on_device(out_grad, layer_input, gate_pre, up_pre, down_weight, proj_hidden, proj_model, example_ids):
    hproj = proj_hidden.T
    up1 = lax.ppermute(down_weight, "y", turn(NY, 1))
    dn1 = lax.ppermute(down_weight, "y", turn(NY, -1))
    p1, p2, p3, early = prepare(out_grad, gate_pre, up_pre, layer_input, proj_model, hproj, down_weight.shape[1])
    up1, dn1, early = lax.optimization_barrier((up1, dn1, early))
    x1, x2, x3 = [lax.ppermute(p, "x", turn(NX, s + 1)) for s, p in enumerate((p1, p2, p3))]
    up2 = lax.ppermute(up1, "y", turn(NY, 1))
    dn2 = lax.ppermute(dn1, "y", turn(NY, -1))
    got = lax.all_to_all(early, ZC, 0, 0)
    up2, dn2, x2 = lax.optimization_barrier((up2, dn2, x2))
    up3 = lax.ppermute(up2, "y", turn(NY, 1))
    dn3 = lax.ppermute(dn2, "y", turn(NY, -1))
    up3, dn3 = lax.optimization_barrier((up3, dn3))
    w4 = lax.ppermute(up3, "y", turn(NY, 1))
    o2 = lax.ppermute(x2, "core", turn(NC, 1))
    o2, x1, x3, w4 = lax.optimization_barrier((o2, x1, x3, w4))
    up_part = main(out_grad, gate_pre, (x1, x2, x3, o2), (down_weight, up1, up2, up3, w4, dn3, dn2, dn1), hproj)
    up_part, got = lax.optimization_barrier((up_part, got))
    up_side = lax.all_to_all(up_part.reshape((NX * NB,) + up_part.shape[2:]), ("x",) + ZC, 0, 0)
    mine, hid_side = settle(got, up_part.shape[2])
    other = lax.ppermute(mine, "core", turn(NC, 1))
    return tuple(finish(up_side, hid_side, mine, other, example_ids))


def solution(mesh):
    fine = Mesh(mesh.devices.reshape(NY, NX, NZ, NC), ("y", "x", "z", "core"))
    yx = ("y", "x")
    in_specs = (P(yx, None), P(yx, ZC), P(yx, ZC), P(yx, ZC), P(ZC, yx), P(ZC, None), P(ZC, None), P(yx, None))
    out_specs = (P(yx, ZC), P(yx, ZC))
    return jax.shard_map(on_device, mesh=fine, in_specs=in_specs, out_specs=out_specs, check_vma=False)
```

```python
import jax
import jax.numpy as jnp
from jax import lax
from jax.experimental import pallas as pl
from jax.experimental.pallas import tpu as pltpu
from jax.sharding import Mesh
from jax.sharding import PartitionSpec as P

NY, NX, NZ, NC = 8, 4, 8, 2
NB = NZ * NC
HALF = NY // NC
EXTRA = 16
ZC = ("z", "core")
BF16, F32 = jnp.bfloat16, jnp.float32
HBM = pl.BlockSpec(memory_space=pltpu.HBM)
VMEM = pl.BlockSpec(memory_space=pltpu.VMEM)
WIDE = pltpu.CompilerParams(vmem_limit_bytes=60 << 20)


def turn(n, step):
    return [(i, (i + step) % n) for i in range(n)]


def dot_nt(a, b, **kw):
    return lax.dot_general(a, b, (((1,), (1,)), ((), ())), preferred_element_type=F32, **kw)


def silu(v):
    return v / (1.0 + jnp.exp(-v))


def columns(y, back, x, wide):
    return pl.multiple_of((lax.rem(y - back + NY, NY) * NX + x) * wide, wide)


def here():
    return lax.axis_index("y"), lax.axis_index("x"), lax.axis_index("z") * NC + lax.axis_index("core")


def prepare_kernel(grad, gate, up, inp, model, hproj, p1, p2, p3, early, buf, gate_v, up_v, inp_v, gcols, model_v, hproj_v, in_sem, out_sem, side_sem):
    tok, hid = gate.shape
    feat = inp.shape[1]
    y, x, blk = here()
    core = lax.axis_index("core")
    wide = (p1.shape[1] - hid) // NY
    fills, sends = [], []
    for s, out in ((2, p2), (1, p1), (3, p3)):
        at = lax.rem(x + s, NX)
        size = out.shape[1]
        part = (size - hid) // wide
        first = core * HALF if part < NY else 0
        fill = [pltpu.make_async_copy(gate, buf.at[s - 1, :, pl.ds(0, hid)], in_sem.at[s - 1, NY])]
        for i in range(part):
            fill.append(
                pltpu.make_async_copy(
                    grad.at[:, pl.ds(columns(y, first + i, at, wide), wide)],
                    buf.at[s - 1, :, pl.ds(hid + i * wide, wide)],
                    in_sem.at[s - 1, i],
                )
            )
        fills.append(fill)
        sends.append(pltpu.make_async_copy(buf.at[s - 1, :, pl.ds(0, size)], out, out_sem.at[s - 1]))
        for c in fill:
            c.start()
    loads = [
        pltpu.make_async_copy(gate, gate_v, side_sem.at[0]),
        pltpu.make_async_copy(up, up_v, side_sem.at[1]),
        pltpu.make_async_copy(inp, inp_v, side_sem.at[2]),
        pltpu.make_async_copy(grad.at[:, pl.ds(pl.multiple_of(blk * feat, feat), feat)], gcols, side_sem.at[3]),
        pltpu.make_async_copy(model, model_v, side_sem.at[4]),
        pltpu.make_async_copy(hproj, hproj_v, side_sem.at[5]),
    ]
    for c in loads:
        c.start()
    for fill, send in zip(fills, sends):
        for c in fill:
            c.wait()
        send.start()
    for c in loads:
        c.wait()
    hidden = (silu(gate_v[...].astype(F32)) * up_v[...].astype(F32)).astype(BF16)
    hid_side = dot_nt(hproj_v[...], hidden)
    high = hid_side.astype(BF16).astype(F32)
    low = hid_side - high
    m = model_v[...]
    side = jnp.concatenate(
        [jnp.dot(v[...], m, preferred_element_type=F32) for v in (gcols, inp_v)], axis=1
    ).astype(BF16)
    width = side.shape[1]
    per = hproj.shape[0] // NB
    half = tok // NC
    for b in range(NB):
        early[b, 0:half, :] = side[(b % NC) * half : (b % NC + 1) * half]
        rows = jnp.concatenate(
            [high[b * per : (b + 1) * per], low[b * per : (b + 1) * per], jnp.zeros((EXTRA - 2 * per, tok), F32)], axis=0
        )
        early[b, half : half + EXTRA, :] = jnp.concatenate(
            [rows, jnp.zeros((EXTRA, width - tok), F32)], axis=1
        ).astype(BF16)
    for c in sends:
        c.wait()


def prepare(grad, gate, up, inp, model, hproj, wide):
    tok, hid = gate.shape
    feat = inp.shape[1]
    full, part = [jax.ShapeDtypeStruct((tok, hid + n * wide), BF16) for n in (NY, HALF)]
    return pl.pallas_call(
        prepare_kernel,
        out_shape=[full, part, full] + [jax.ShapeDtypeStruct((NB, tok // NC + EXTRA, 2 * model.shape[1]), BF16)],
        in_specs=[HBM] * 6,
        out_specs=[HBM] * 3 + [VMEM],
        scratch_shapes=[
            pltpu.VMEM((NX - 1, tok, hid + NY * wide), BF16),
            pltpu.VMEM((tok, hid), BF16),
            pltpu.VMEM((tok, hid), BF16),
            pltpu.VMEM((tok, feat), BF16),
            pltpu.VMEM((tok, feat), BF16),
            pltpu.VMEM(model.shape, BF16),
            pltpu.VMEM(hproj.shape, BF16),
            pltpu.SemaphoreType.DMA((NX - 1, NY + 1)),
            pltpu.SemaphoreType.DMA((NX - 1,)),
            pltpu.SemaphoreType.DMA((6,)),
        ],
        compiler_params=WIDE,
        cost_estimate=pl.CostEstimate(flops=80_000_000, bytes_accessed=8_000_000, transcendentals=tok * hid),
        name="prepare",
    )(grad, gate, up, inp, model, hproj)


def near_kernel(grad, own, x1, x2, x3, o2, w0, w1, w2, w3, w5, w6, w7, acc, last, gate, g, w, g_sem, w_sem, gate_sem):
    y, x, _ = here()
    core = lax.axis_index("core")
    nx, tok, hid = acc.shape
    wide = w0.shape[1]
    n = HALF * wide
    near = pl.ds(pl.multiple_of(core * n, n), n)
    away = pl.ds(pl.multiple_of((1 - core) * n, n), n)
    copies = []
    for i in range(NY):
        copies.append(
            pltpu.make_async_copy(
                grad.at[:, pl.ds(columns(y, i, x, wide), wide)], g.at[0, :, pl.ds(i * wide, wide)], g_sem.at[0, i]
            )
        )
    for s, got in ((1, x1), (3, x3)):
        copies.append(pltpu.make_async_copy(got.at[:, pl.ds(hid, NY * wide)], g.at[s], g_sem.at[s, 0]))
    copies.append(pltpu.make_async_copy(x2.at[:, pl.ds(hid, n)], g.at[2, :, near], g_sem.at[2, 0]))
    copies.append(pltpu.make_async_copy(o2.at[:, pl.ds(hid, n)], g.at[2, :, away], g_sem.at[2, 1]))
    for i, src in enumerate((w0, w1, w2, w3, w5, w6, w7)):
        copies.append(pltpu.make_async_copy(src, w.at[:, pl.ds(i * wide, wide)], w_sem.at[i]))
    gates = [pltpu.make_async_copy(own, gate.at[0], gate_sem.at[0])]
    for s, got in enumerate((x1, x2, x3)):
        gates.append(pltpu.make_async_copy(got.at[:, pl.ds(0, hid)], gate.at[s + 1], gate_sem.at[s + 1]))
    for c in copies + gates:
        c.start()
    for c in copies:
        c.wait()
    low = g[:, :, 0:n].reshape(nx * tok, n)
    high = g[:, :, n + wide :].reshape(nx * tok, n - wide)
    gh = dot_nt(low, w[:, 0:n]) + dot_nt(high, w[:, n:])
    acc[...] = gh.reshape(nx, tok, hid)
    last[...] = g[:, :, n : n + wide]
    for c in gates:
        c.wait()


def near(grad, own, got, shards):
    tok = grad.shape[0]
    hid, wide = shards[0].shape
    k = (NY - 1) * wide
    return pl.pallas_call(
        near_kernel,
        out_shape=[
            jax.ShapeDtypeStruct((NX, tok, hid), F32),
            jax.ShapeDtypeStruct((NX, tok, wide), BF16),
            jax.ShapeDtypeStruct((NX, tok, hid), BF16),
        ],
        in_specs=[HBM] * 13,
        out_specs=[VMEM] * 3,
        scratch_shapes=[
            pltpu.VMEM((NX, tok, NY * wide), BF16),
            pltpu.VMEM((hid, k), BF16),
            pltpu.SemaphoreType.DMA((NX, NY)),
            pltpu.SemaphoreType.DMA((NY - 1,)),
            pltpu.SemaphoreType.DMA((NX,)),
        ],
        compiler_params=pltpu.CompilerParams(vmem_limit_bytes=50 << 20),
        cost_estimate=pl.CostEstimate(flops=1_000_000, bytes_accessed=100_000, transcendentals=0),
        name="near",
    )(grad, own, *got, *shards)


def far_kernel(acc, last, gates, w4, proj, out, a_v, g, gate, w, p, sems):
    _, x, _ = here()
    nx, tok, hid = acc.shape
    per = proj.shape[0] // NB
    heads = [
        pltpu.make_async_copy(w4, w, sems.at[nx, 0]),
        pltpu.make_async_copy(last, g, sems.at[nx, 1]),
        pltpu.make_async_copy(proj, p, sems.at[nx, 2]),
    ]
    waits = []
    for s in range(nx):
        waits.append(
            [
                pltpu.make_async_copy(acc.at[s], a_v.at[s], sems.at[s, 0]),
                pltpu.make_async_copy(gates.at[s], gate.at[s], sems.at[s, 1]),
            ]
        )
    for c in heads:
        c.start()
    for pair in waits:
        for c in pair:
            c.start()
    for c in heads:
        c.wait()
    for s in range(nx):
        for c in waits[s]:
            c.wait()
        gu = (a_v[s] + dot_nt(g[s], w[...])) * silu(gate[s].astype(F32))
        hi = gu.astype(BF16)
        lo = (gu - hi.astype(F32)).astype(BF16)
        total = dot_nt(p[...], hi) + dot_nt(p[...], lo)
        to = lax.rem(x - s + nx, nx)
        for b in range(NB):
            out[to, b] = total[b * per : (b + 1) * per, :]


def far(acc, last, gates, w4, proj):
    nx, tok, hid = acc.shape
    wide = w4.shape[1]
    per = proj.shape[0] // NB
    return pl.pallas_call(
        far_kernel,
        out_shape=jax.ShapeDtypeStruct((nx, NB, per, tok), F32),
        in_specs=[HBM] * 5,
        out_specs=VMEM,
        scratch_shapes=[
            pltpu.VMEM((nx, tok, hid), F32),
            pltpu.VMEM((nx, tok, wide), BF16),
            pltpu.VMEM((nx, tok, hid), BF16),
            pltpu.VMEM((hid, wide), BF16),
            pltpu.VMEM(proj.shape, BF16),
            pltpu.SemaphoreType.DMA((nx + 1, 3)),
        ],
        compiler_params=pltpu.CompilerParams(vmem_limit_bytes=50 << 20),
        cost_estimate=pl.CostEstimate(
            flops=7 * nx * tok * hid * (NY * wide + 128), bytes_accessed=9_000_000, transcendentals=nx * tok * hid
        ),
        name="far",
    )(acc, last, gates, w4, proj)


def score(left, right, which, out):
    picked = jnp.concatenate([jnp.where(which == e, left, 0.0) for e in range(2)], axis=0)
    res = jnp.dot(picked, right, precision=lax.Precision.HIGHEST, preferred_element_type=F32)
    per, width = left.shape[0], right.shape[1]
    for e in range(2):
        for k in range(per):
            out[e : e + 1, k * width : (k + 1) * width] = res[e * per + k : e * per + k + 1, :]


def settle_kernel(got, side, hid_side):
    total = got[0].astype(F32)
    for b in range(1, NB):
        total = total + got[b].astype(F32)
    half = side.shape[0]
    per, tok = hid_side.shape
    side[...] = total[:half]
    hid_side[...] = total[half : half + per, 0:tok] + total[half + per : half + 2 * per, 0:tok]


def settle(got, per):
    _, rows, width = got.shape
    half = rows - EXTRA
    return pl.pallas_call(
        settle_kernel,
        out_shape=[jax.ShapeDtypeStruct((half, width), F32), jax.ShapeDtypeStruct((per, half * NC), F32)],
        in_specs=[VMEM],
        out_specs=[VMEM, VMEM],
        name="settle",
    )(got)


def finish_kernel(got, hid_side, mine, other, ids, down, up):
    first = lax.axis_index("core") == 0
    side = jnp.concatenate(
        [jnp.where(first, mine[...], other[...]), jnp.where(first, other[...], mine[...])], axis=0
    )
    width = side.shape[1] // 2
    parts = [got[b] for b in range(got.shape[0])]
    while len(parts) > 1:
        parts = [parts[i] + parts[i + 1] for i in range(0, len(parts), 2)]
    score(hid_side[...], side[:, :width], ids[...], down)
    score(parts[0], side[:, width:], ids[...], up)


def finish(got, hid_side, mine, other, ids):
    out = jax.ShapeDtypeStruct((2, got.shape[1] * mine.shape[1] // 2), F32)
    return pl.pallas_call(
        finish_kernel, out_shape=[out, out], in_specs=[VMEM] * 5, out_specs=[VMEM, VMEM], name="finish"
    )(got, hid_side, mine, other, ids)


def on_device(out_grad, layer_input, gate_pre, up_pre, down_weight, proj_hidden, proj_model, example_ids):
    hproj = proj_hidden.T
    up1 = lax.ppermute(down_weight, "y", turn(NY, 1))
    dn1 = lax.ppermute(down_weight, "y", turn(NY, -1))
    p1, p2, p3, early = prepare(out_grad, gate_pre, up_pre, layer_input, proj_model, hproj, down_weight.shape[1])
    up1, dn1, early = lax.optimization_barrier((up1, dn1, early))
    x1, x2, x3 = [lax.ppermute(p, "x", turn(NX, s + 1)) for s, p in enumerate((p1, p2, p3))]
    up2 = lax.ppermute(up1, "y", turn(NY, 1))
    dn2 = lax.ppermute(dn1, "y", turn(NY, -1))
    got = lax.all_to_all(early, ZC, 0, 0)
    up2, dn2, x2 = lax.optimization_barrier((up2, dn2, x2))
    up3 = lax.ppermute(up2, "y", turn(NY, 1))
    dn3 = lax.ppermute(dn2, "y", turn(NY, -1))
    up3, dn3 = lax.optimization_barrier((up3, dn3))
    w4 = lax.ppermute(up3, "y", turn(NY, 1))
    o2 = lax.ppermute(x2, "core", turn(NC, 1))
    o2, x1, x3 = lax.optimization_barrier((o2, x1, x3))
    acc, last, gates = near(out_grad, gate_pre, (x1, x2, x3, o2), (down_weight, up1, up2, up3, dn3, dn2, dn1))
    up_part = far(acc, last, gates, w4, hproj)
    up_part, got = lax.optimization_barrier((up_part, got))
    up_side = lax.all_to_all(up_part.reshape((NX * NB,) + up_part.shape[2:]), ("x",) + ZC, 0, 0)
    mine, hid_side = settle(got, up_part.shape[2])
    other = lax.ppermute(mine, "core", turn(NC, 1))
    return tuple(finish(up_side, hid_side, mine, other, example_ids))


def solution(mesh):
    fine = Mesh(mesh.devices.reshape(NY, NX, NZ, NC), ("y", "x", "z", "core"))
    yx = ("y", "x")
    in_specs = (P(yx, None), P(yx, ZC), P(yx, ZC), P(yx, ZC), P(ZC, yx), P(ZC, None), P(ZC, None), P(yx, None))
    out_specs = (P(yx, ZC), P(yx, ZC))
    return jax.shard_map(on_device, mesh=fine, in_specs=in_specs, out_specs=out_specs, check_vma=False)
```

```python
import jax
import jax.numpy as jnp
from jax import lax
from jax.experimental import pallas as pl
from jax.experimental.pallas import tpu as pltpu
from jax.sharding import Mesh
from jax.sharding import PartitionSpec as P

NY, NX, NZ, NC = 8, 4, 8, 2
NB = NZ * NC
HALF = NY // NC
EXTRA = 16
ZC = ("z", "core")
BF16, F32 = jnp.bfloat16, jnp.float32
HBM = pl.BlockSpec(memory_space=pltpu.HBM)
VMEM = pl.BlockSpec(memory_space=pltpu.VMEM)
WIDE = pltpu.CompilerParams(vmem_limit_bytes=60 << 20)


def turn(n, step):
    return [(i, (i + step) % n) for i in range(n)]


def dot_nt(a, b, **kw):
    return lax.dot_general(a, b, (((1,), (1,)), ((), ())), preferred_element_type=F32, **kw)


def silu(v):
    return v / (1.0 + jnp.exp(-v))


def columns(y, back, x, wide):
    return pl.multiple_of((lax.rem(y - back + NY, NY) * NX + x) * wide, wide)


def here():
    return lax.axis_index("y"), lax.axis_index("x"), lax.axis_index("z") * NC + lax.axis_index("core")


def prepare_kernel(grad, gate, up, inp, model, hproj, p1, p2, p3, early, buf, gate_v, up_v, inp_v, gcols, model_v, hproj_v, in_sem, out_sem, side_sem):
    tok, hid = gate.shape
    feat = inp.shape[1]
    y, x, blk = here()
    core = lax.axis_index("core")
    wide = (p1.shape[1] - hid) // NY
    fills, sends = [], []
    for s, out in ((2, p2), (1, p1), (3, p3)):
        at = lax.rem(x + s, NX)
        size = out.shape[1]
        part = (size - hid) // wide
        first = core * HALF if part < NY else 0
        fill = [pltpu.make_async_copy(gate, buf.at[s - 1, :, pl.ds(0, hid)], in_sem.at[s - 1, NY])]
        for i in range(part):
            fill.append(
                pltpu.make_async_copy(
                    grad.at[:, pl.ds(columns(y, first + i, at, wide), wide)],
                    buf.at[s - 1, :, pl.ds(hid + i * wide, wide)],
                    in_sem.at[s - 1, i],
                )
            )
        fills.append(fill)
        sends.append(pltpu.make_async_copy(buf.at[s - 1, :, pl.ds(0, size)], out, out_sem.at[s - 1]))
        for c in fill:
            c.start()
    loads = [
        pltpu.make_async_copy(gate, gate_v, side_sem.at[0]),
        pltpu.make_async_copy(up, up_v, side_sem.at[1]),
        pltpu.make_async_copy(inp, inp_v, side_sem.at[2]),
        pltpu.make_async_copy(grad.at[:, pl.ds(pl.multiple_of(blk * feat, feat), feat)], gcols, side_sem.at[3]),
        pltpu.make_async_copy(model, model_v, side_sem.at[4]),
        pltpu.make_async_copy(hproj, hproj_v, side_sem.at[5]),
    ]
    for c in loads:
        c.start()
    for fill, send in zip(fills, sends):
        for c in fill:
            c.wait()
        send.start()
    for c in loads:
        c.wait()
    hidden = (silu(gate_v[...].astype(F32)) * up_v[...].astype(F32)).astype(BF16)
    hid_side = dot_nt(hproj_v[...], hidden)
    high = hid_side.astype(BF16).astype(F32)
    low = hid_side - high
    m = model_v[...]
    side = jnp.concatenate(
        [jnp.dot(v[...], m, preferred_element_type=F32) for v in (gcols, inp_v)], axis=1
    ).astype(BF16)
    width = side.shape[1]
    per = hproj.shape[0] // NB
    half = tok // NC
    for b in range(NB):
        early[b, 0:half, :] = side[(b % NC) * half : (b % NC + 1) * half]
        rows = jnp.concatenate(
            [high[b * per : (b + 1) * per], low[b * per : (b + 1) * per], jnp.zeros((EXTRA - 2 * per, tok), F32)], axis=0
        )
        early[b, half : half + EXTRA, :] = jnp.concatenate(
            [rows, jnp.zeros((EXTRA, width - tok), F32)], axis=1
        ).astype(BF16)
    for c in sends:
        c.wait()


def prepare(grad, gate, up, inp, model, hproj, wide):
    tok, hid = gate.shape
    feat = inp.shape[1]
    full, part = [jax.ShapeDtypeStruct((tok, hid + n * wide), BF16) for n in (NY, HALF)]
    return pl.pallas_call(
        prepare_kernel,
        out_shape=[full, part, full] + [jax.ShapeDtypeStruct((NB, tok // NC + EXTRA, 2 * model.shape[1]), BF16)],
        in_specs=[HBM] * 6,
        out_specs=[HBM] * 3 + [VMEM],
        scratch_shapes=[
            pltpu.VMEM((NX - 1, tok, hid + NY * wide), BF16),
            pltpu.VMEM((tok, hid), BF16),
            pltpu.VMEM((tok, hid), BF16),
            pltpu.VMEM((tok, feat), BF16),
            pltpu.VMEM((tok, feat), BF16),
            pltpu.VMEM(model.shape, BF16),
            pltpu.VMEM(hproj.shape, BF16),
            pltpu.SemaphoreType.DMA((NX - 1, NY + 1)),
            pltpu.SemaphoreType.DMA((NX - 1,)),
            pltpu.SemaphoreType.DMA((6,)),
        ],
        compiler_params=WIDE,
        cost_estimate=pl.CostEstimate(flops=80_000_000, bytes_accessed=8_000_000, transcendentals=tok * hid),
        name="prepare",
    )(grad, gate, up, inp, model, hproj)


def near_kernel(grad, own, x1, x2, x3, o2, w0, w1, w2, w3, w5, w6, w7, acc, last, gate, g, w, g_sem, w_sem, gate_sem):
    y, x, _ = here()
    core = lax.axis_index("core")
    nx, tok, hid = acc.shape
    wide = w0.shape[1]
    n = HALF * wide
    near = pl.ds(pl.multiple_of(core * n, n), n)
    away = pl.ds(pl.multiple_of((1 - core) * n, n), n)
    copies = []
    for i in range(NY):
        copies.append(
            pltpu.make_async_copy(
                grad.at[:, pl.ds(columns(y, i, x, wide), wide)], g.at[0, :, pl.ds(i * wide, wide)], g_sem.at[0, i]
            )
        )
    for s, got in ((1, x1), (3, x3)):
        copies.append(pltpu.make_async_copy(got.at[:, pl.ds(hid, NY * wide)], g.at[s], g_sem.at[s, 0]))
    copies.append(pltpu.make_async_copy(x2.at[:, pl.ds(hid, n)], g.at[2, :, near], g_sem.at[2, 0]))
    copies.append(pltpu.make_async_copy(o2.at[:, pl.ds(hid, n)], g.at[2, :, away], g_sem.at[2, 1]))
    for i, src in enumerate((w0, w1, w2, w3, w5, w6, w7)):
        copies.append(pltpu.make_async_copy(src, w.at[:, pl.ds(i * wide, wide)], w_sem.at[i]))
    gates = [pltpu.make_async_copy(own, gate.at[0], gate_sem.at[0])]
    for s, got in enumerate((x1, x2, x3)):
        gates.append(pltpu.make_async_copy(got.at[:, pl.ds(0, hid)], gate.at[s + 1], gate_sem.at[s + 1]))
    for c in copies + gates:
        c.start()
    for c in copies:
        c.wait()
    low = g[:, :, 0:n].reshape(nx * tok, n)
    high = g[:, :, n + wide :].reshape(nx * tok, n - wide)
    gh = dot_nt(low, w[:, 0:n]) + dot_nt(high, w[:, n:])
    acc[...] = gh.reshape(nx, tok, hid)
    last[...] = g[:, :, n : n + wide]
    for c in gates:
        c.wait()


def near(grad, own, got, shards):
    tok = grad.shape[0]
    hid, wide = shards[0].shape
    k = (NY - 1) * wide
    return pl.pallas_call(
        near_kernel,
        out_shape=[
            jax.ShapeDtypeStruct((NX, tok, hid), F32),
            jax.ShapeDtypeStruct((NX, tok, wide), BF16),
            jax.ShapeDtypeStruct((NX, tok, hid), BF16),
        ],
        in_specs=[HBM] * 13,
        out_specs=[VMEM] * 3,
        scratch_shapes=[
            pltpu.VMEM((NX, tok, NY * wide), BF16),
            pltpu.VMEM((hid, k), BF16),
            pltpu.SemaphoreType.DMA((NX, NY)),
            pltpu.SemaphoreType.DMA((NY - 1,)),
            pltpu.SemaphoreType.DMA((NX,)),
        ],
        compiler_params=pltpu.CompilerParams(vmem_limit_bytes=50 << 20),
        cost_estimate=pl.CostEstimate(flops=1_000_000, bytes_accessed=100_000, transcendentals=0),
        name="near",
    )(grad, own, *got, *shards)


def far_kernel(acc, last, gates, w4, proj, out, a_v, g, gate, w, p, sems):
    _, x, _ = here()
    nx, tok, hid = acc.shape
    per = proj.shape[0] // NB
    heads = [
        pltpu.make_async_copy(w4, w, sems.at[nx, 0]),
        pltpu.make_async_copy(last, g, sems.at[nx, 1]),
        pltpu.make_async_copy(proj, p, sems.at[nx, 2]),
    ]
    waits = []
    for s in range(nx):
        waits.append(
            [
                pltpu.make_async_copy(acc.at[s], a_v.at[s], sems.at[s, 0]),
                pltpu.make_async_copy(gates.at[s], gate.at[s], sems.at[s, 1]),
            ]
        )
    for c in heads:
        c.start()
    for pair in waits:
        for c in pair:
            c.start()
    for c in heads:
        c.wait()
    for s in range(nx):
        for c in waits[s]:
            c.wait()
        gu = (a_v[s] + dot_nt(g[s], w[...])) * silu(gate[s].astype(F32))
        hi = gu.astype(BF16)
        lo = (gu - hi.astype(F32)).astype(BF16)
        total = dot_nt(p[...], hi) + dot_nt(p[...], lo)
        to = lax.rem(x - s + nx, nx)
        for b in range(NB):
            out[b, to] = total[b * per : (b + 1) * per, :]


def far(acc, last, gates, w4, proj):
    nx, tok, hid = acc.shape
    wide = w4.shape[1]
    per = proj.shape[0] // NB
    return pl.pallas_call(
        far_kernel,
        out_shape=jax.ShapeDtypeStruct((NB, nx, per, tok), F32),
        in_specs=[HBM] * 5,
        out_specs=VMEM,
        scratch_shapes=[
            pltpu.VMEM((nx, tok, hid), F32),
            pltpu.VMEM((nx, tok, wide), BF16),
            pltpu.VMEM((nx, tok, hid), BF16),
            pltpu.VMEM((hid, wide), BF16),
            pltpu.VMEM(proj.shape, BF16),
            pltpu.SemaphoreType.DMA((nx + 1, 3)),
        ],
        compiler_params=pltpu.CompilerParams(vmem_limit_bytes=50 << 20),
        cost_estimate=pl.CostEstimate(
            flops=7 * nx * tok * hid * (NY * wide + 128), bytes_accessed=9_000_000, transcendentals=nx * tok * hid
        ),
        name="far",
    )(acc, last, gates, w4, proj)


def score(left, right, which, out):
    picked = jnp.concatenate([jnp.where(which == e, left, 0.0) for e in range(2)], axis=0)
    res = jnp.dot(picked, right, precision=lax.Precision.HIGHEST, preferred_element_type=F32)
    per, width = left.shape[0], right.shape[1]
    for e in range(2):
        for k in range(per):
            out[e : e + 1, k * width : (k + 1) * width] = res[e * per + k : e * per + k + 1, :]


def settle_kernel(got, side, hid_side):
    total = got[0].astype(F32)
    for b in range(1, NB):
        total = total + got[b].astype(F32)
    half = side.shape[0]
    per, tok = hid_side.shape
    side[...] = total[:half]
    hid_side[...] = total[half : half + per, 0:tok] + total[half + per : half + 2 * per, 0:tok]


def settle(got, per):
    _, rows, width = got.shape
    half = rows - EXTRA
    return pl.pallas_call(
        settle_kernel,
        out_shape=[jax.ShapeDtypeStruct((half, width), F32), jax.ShapeDtypeStruct((per, half * NC), F32)],
        in_specs=[VMEM],
        out_specs=[VMEM, VMEM],
        name="settle",
    )(got)


def finish_kernel(got, hid_side, mine, other, ids, down, up):
    first = lax.axis_index("core") == 0
    side = jnp.concatenate(
        [jnp.where(first, mine[...], other[...]), jnp.where(first, other[...], mine[...])], axis=0
    )
    width = side.shape[1] // 2
    parts = [got[b] for b in range(got.shape[0])]
    while len(parts) > 1:
        parts = [parts[i] + parts[i + 1] for i in range(0, len(parts), 2)]
    score(hid_side[...], side[:, :width], ids[...], down)
    score(parts[0], side[:, width:], ids[...], up)


def finish(got, hid_side, mine, other, ids):
    out = jax.ShapeDtypeStruct((2, got.shape[1] * mine.shape[1] // 2), F32)
    return pl.pallas_call(
        finish_kernel, out_shape=[out, out], in_specs=[VMEM] * 5, out_specs=[VMEM, VMEM], name="finish"
    )(got, hid_side, mine, other, ids)


def on_device(out_grad, layer_input, gate_pre, up_pre, down_weight, proj_hidden, proj_model, example_ids):
    hproj = proj_hidden.T
    up1 = lax.ppermute(down_weight, "y", turn(NY, 1))
    dn1 = lax.ppermute(down_weight, "y", turn(NY, -1))
    p1, p2, p3, early = prepare(out_grad, gate_pre, up_pre, layer_input, proj_model, hproj, down_weight.shape[1])
    up1, dn1, early = lax.optimization_barrier((up1, dn1, early))
    x1, x2, x3 = [lax.ppermute(p, "x", turn(NX, s + 1)) for s, p in enumerate((p1, p2, p3))]
    up2 = lax.ppermute(up1, "y", turn(NY, 1))
    dn2 = lax.ppermute(dn1, "y", turn(NY, -1))
    got = lax.all_to_all(early, ZC, 0, 0)
    up2, dn2, x2 = lax.optimization_barrier((up2, dn2, x2))
    up3 = lax.ppermute(up2, "y", turn(NY, 1))
    dn3 = lax.ppermute(dn2, "y", turn(NY, -1))
    up3, dn3 = lax.optimization_barrier((up3, dn3))
    w4 = lax.ppermute(up3, "y", turn(NY, 1))
    o2 = lax.ppermute(x2, "core", turn(NC, 1))
    o2, x1, x3 = lax.optimization_barrier((o2, x1, x3))
    acc, last, gates = near(out_grad, gate_pre, (x1, x2, x3, o2), (down_weight, up1, up2, up3, dn3, dn2, dn1))
    up_part = far(acc, last, gates, w4, hproj)
    up_part, got = lax.optimization_barrier((up_part, got))
    up_side = lax.all_to_all(up_part.reshape((NX * NB,) + up_part.shape[2:]), ZC + ("x",), 0, 0)
    mine, hid_side = settle(got, up_part.shape[2])
    other = lax.ppermute(mine, "core", turn(NC, 1))
    return tuple(finish(up_side, hid_side, mine, other, example_ids))


def solution(mesh):
    fine = Mesh(mesh.devices.reshape(NY, NX, NZ, NC), ("y", "x", "z", "core"))
    yx = ("y", "x")
    in_specs = (P(yx, None), P(yx, ZC), P(yx, ZC), P(yx, ZC), P(ZC, yx), P(ZC, None), P(ZC, None), P(yx, None))
    out_specs = (P(yx, ZC), P(yx, ZC))
    return jax.shard_map(on_device, mesh=fine, in_specs=in_specs, out_specs=out_specs, check_vma=False)
```
